256 devices in a mesh: bricks: 64 (over y, z, core), pts: 4 (over x).
Axes of the slice: x: 4, y: 4, z: 8, core: 2. Of those that a mesh axis runs over, the one named last changes fastest.
Arguments:
- right_side: float32 [1024, 64, 128], P(('bricks', 'pts'))
- initial_guess: float32 [1024, 64, 128], P(('bricks', 'pts')), may hold values from -3 to 3
- point_cell: int32 [3, 524288], P(None, ('bricks', 'pts')), may hold values from 1 to 126, as said below
- point_offset: float32 [3, 524288], P(None, ('bricks', 'pts')), may hold values from -0.5 to 0.5
- point_weight: float32 [524288], P(('bricks', 'pts')), may hold values from 1 to 8
- point_mask: int32 [524288], P(('bricks', 'pts')), may hold values from 0 to 1, as said below
- block_count: int32 [256], P(('bricks', 'pts')), may hold values from 1 to 8, as said below
Outputs:
- solution_field: float32 [1024, 64, 128], P(('bricks', 'pts'))
- residual: float32 [1024, 64, 128], P(('bricks', 'pts'))
The draws below stay inside these ranges and needn't reach their ends.
Inputs may be any that keep to these rules, and one draw needn't show every extreme that they name: `point_cell`: component 0 lies in 1 to 2, component 1 in 1 to 62, component 2 in 1 to 126, so that every point's 27 cells lie in its own device's slab. `point_mask`: within each aligned block of 256 points the ones come first. `block_count`: some device has all 8 blocks live in every draw.
All inputs are finite; a program needn't handle non-finite values.
Results may differ from the reference program's by a relative error of at most 0.0035.
Values sent between devices are 32-bit elements; how exact they have to be, the bound alone decides.
A program may use at most 64 MiB of HBM per device.

```python
import math
import jax
import jax.numpy as jnp
from jax import lax

GX = 4
GY = 64
GZ = 128
BLOCKS_DEV = 8
BLOCK = 256
ITERS = 2
NDEV = 256
NX = 1024
PTS_DEV = 2048
PTS = 524288


def draw_right_side(key, part):
    key = jax.random.fold_in(key, 11)
    ramp = jnp.arange(NX, dtype=jnp.float32) / (NX - 1)
    factor = jnp.exp(jnp.log(3.0) * ramp)[:, None, None]
    rough = jnp.clip(jax.random.normal(key, (NX, GY, GZ), jnp.float32), -6.0, 6.0)
    return rough * factor


def draw_point_cell(key, part):
    key = jax.random.fold_in(key, 12)
    key_x, key_y, key_z = jax.random.split(key, 3)
    cell_x = jax.random.randint(key_x, (PTS,), 1, GX - 1)
    cell_y = jax.random.randint(key_y, (PTS,), 1, GY - 1)
    cell_z = jax.random.randint(key_z, (PTS,), 1, GZ - 1)
    return jnp.stack([cell_x, cell_y, cell_z]).astype(jnp.int32)


def draw_point_mask(key, part):
    key = jax.random.fold_in(key, 13)
    fills = jax.random.randint(key, (PTS // BLOCK,), 96, BLOCK + 1)
    position = jnp.arange(PTS, dtype=jnp.int32)
    return (position % BLOCK < fills[position // BLOCK]).astype(jnp.int32)


def draw_block_count(key, part):
    key = jax.random.fold_in(key, 14)
    shift_key, trim_key, top_key = jax.random.split(key, 3)
    shifts = jax.random.randint(shift_key, (NDEV,), 0, 4)
    reduced = jnp.maximum(jnp.right_shift(jnp.full((NDEV,), BLOCKS_DEV, jnp.int32), shifts), 1)
    trims = jax.random.randint(trim_key, (NDEV,), 0, BLOCKS_DEV + 1)
    trimmed = reduced - trims % (reduced // 2 + 1)
    fullest = jax.random.randint(top_key, (), 0, NDEV)
    return jnp.where(jnp.arange(NDEV, dtype=jnp.int32) == fullest, BLOCKS_DEV, trimmed).astype(jnp.int32)


def level_of(key, shape, cuts, least, largest):
    def one(dim, parts):
        steps = jax.random.uniform(jax.random.fold_in(jax.random.fold_in(key, 6), dim), (parts,), jnp.float32, least / len(cuts), largest / len(cuts))
        return jnp.repeat(jnp.exp(steps), shape[dim] // parts).reshape((-1,) + (1,) * (len(shape) - dim - 1))

    loudness = one(*cuts[0])
    for cut in cuts[1:]:
        loudness = loudness * one(*cut)
    return loudness


def bell_draw(own_key, dims, spread, most, cuts=(), kind=jnp.bfloat16):
    result = spread * jax.random.normal(own_key, dims, jnp.float32)
    if cuts:
        result = result * level_of(own_key, dims, cuts, -0.22, 0.18)
    return jnp.clip(result, -most, most).astype(kind)


def setup_inputs(seed: int = 0) -> dict:
    key_list = jax.random.split(jax.random.key(seed), 8)
    return {
        "right_side": draw_right_side(jax.random.fold_in(key_list[7], 71), 0),
        "initial_guess": bell_draw(key_list[1], (NX, GY, GZ), 0.5, 3.0, ((0, 256),), jnp.float32),
        "point_cell": draw_point_cell(jax.random.fold_in(key_list[7], 71), 0),
        "point_offset": jnp.clip(jax.random.uniform(key_list[3], (3, PTS), jnp.float32, -0.5, 0.5) * level_of(key_list[3], (3, PTS), ((1, 256),), -0.4, 0.0), -0.5, 0.5),
        "point_weight": jnp.clip(jnp.exp(math.log(8.0) - 2.0794415 * jax.random.uniform(key_list[4], (PTS,), jnp.float32) ** level_of(key_list[4], (PTS,), ((0, 256),), -0.2, 0.2)), 1.0, 8.0),
        "point_mask": draw_point_mask(jax.random.fold_in(key_list[7], 71), 0),
        "block_count": draw_block_count(jax.random.fold_in(key_list[7], 71), 0),
    }


MASS_TAPS = (1.0 / 120.0, 26.0 / 120.0, 66.0 / 120.0, 26.0 / 120.0, 1.0 / 120.0)
STIFF_TAPS = (-1.0 / 6.0, -1.0 / 3.0, 1.0, -1.0 / 3.0, -1.0 / 6.0)


def filter_axis(padded, tap_list, along):
    length = padded.shape[along] - 4
    summed = tap_list[0] * lax.slice_in_dim(padded, 0, length, axis=along)
    for offset in range(1, 5):
        summed = summed + tap_list[offset] * lax.slice_in_dim(padded, offset, offset + length, axis=along)
    return summed


def stencil(extended):
    padded = jnp.pad(extended, ((0, 0), (2, 2), (2, 2)))
    mass_z = filter_axis(padded, MASS_TAPS, 2)
    stiff_z = filter_axis(padded, STIFF_TAPS, 2)
    mass_yz = filter_axis(mass_z, MASS_TAPS, 1)
    cross_yz = filter_axis(mass_z, STIFF_TAPS, 1) + filter_axis(stiff_z, MASS_TAPS, 1)
    return filter_axis(mass_yz, STIFF_TAPS, 0) + filter_axis(cross_yz, MASS_TAPS, 0)


def spline_weights(offset):
    return (0.5 * (0.5 - offset) ** 2, 0.75 - offset * offset, 0.5 * (0.5 + offset) ** 2)


def point_tables(cell_x, cell_y, cell_z, point_offset, span_y, span_z):
    centre = (cell_x * span_y + cell_y) * span_z + cell_z
    factor_x = spline_weights(point_offset[0])
    factor_y = spline_weights(point_offset[1])
    factor_z = spline_weights(point_offset[2])
    index_list = []
    weight_list = []
    for step_x in range(3):
        for step_y in range(3):
            for step_z in range(3):
                index_list.append(centre + ((step_x - 1) * span_y + (step_y - 1)) * span_z + (step_z - 1))
                weight_list.append(factor_x[step_x] * factor_y[step_y] * factor_z[step_z])
    return jnp.stack(index_list).astype(jnp.int32), jnp.stack(weight_list)


def screen(flat_field, indices, weights, strength):
    values = jnp.sum(weights * flat_field[indices], axis=0) * strength
    return jnp.zeros_like(flat_field).at[indices].add(weights * values[None, :])


def reference(right_side, initial_guess, point_cell, point_offset, point_weight, point_mask, block_count):
    device_of = jnp.arange(PTS, dtype=jnp.int32) // PTS_DEV
    block_of = (jnp.arange(PTS, dtype=jnp.int32) % PTS_DEV) // BLOCK
    alive_mask = (block_of < block_count[device_of]) & (point_mask == 1)
    strength = jnp.where(alive_mask, point_weight, jnp.zeros_like(point_weight))
    indices, weights = point_tables(point_cell[0] + device_of * GX, point_cell[1], point_cell[2], point_offset, GY, GZ)

    def operate(vector):
        extended = jnp.pad(vector, ((2, 2), (0, 0), (0, 0)))
        screened = screen(vector.reshape(-1), indices, weights, strength).reshape(vector.shape)
        return stencil(extended) + screened

    solution_field = initial_guess
    residual = right_side - operate(initial_guess)
    direction = residual
    norm_now = jnp.sum(residual * residual)
    for step_index in range(ITERS):
        image = operate(direction)
        alpha = norm_now / jnp.sum(direction * image)
        solution_field = solution_field + alpha * direction
        residual = residual - alpha * image
        norm_next = jnp.sum(residual * residual)
        direction = residual + (norm_next / norm_now) * direction
        norm_now = norm_next
    return solution_field, residual
```

```python
import functools

import jax
import jax.numpy as jnp
from jax import lax
from jax.experimental import pallas as pl
from jax.experimental.pallas import tpu as pltpu
from jax.sharding import PartitionSpec as P

MESH = pl.DeviceIdType.MESH

PLANES = 4
ROWS = 64
COLS = 128
CELLS = PLANES * ROWS
BLOCK = 256
BLOCKS = 8
POINTS = BLOCK * BLOCKS
EDGE = 8

SIZES = {"x": 4, "y": 4, "z": 8, "core": 2}
STAGES = (("x", "y"), ("z", "core"))


def spline_weights(offset):
    return (0.5 * (0.5 - offset) ** 2, 0.75 - offset * offset, 0.5 * (0.5 + offset) ** 2)


def coordinates():
    brick = lax.axis_index("bricks")
    return {
        "x": lax.axis_index("pts"),
        "y": brick // 16,
        "z": (brick // 2) % 8,
        "core": brick % 2,
    }


def device_of(place):
    return ((place["y"] * 8 + place["z"]) * 2 + place["core"], place["x"])


def stage_peers(here, axes):
    steps = [{}]
    for axis in axes:
        steps = [dict(step, **{axis: k}) for step in steps for k in range(SIZES[axis])]
    peers = []
    for step in steps[1:]:
        place = dict(here)
        for axis, k in step.items():
            if k:
                place[axis] = (here[axis] + k) % SIZES[axis]
        peers.append(device_of(place))
    return peers


def two_terms(value):
    high = value.astype(jnp.bfloat16)
    low = (value - high.astype(jnp.float32)).astype(jnp.bfloat16)
    return high, low


def block_row(ref, block):
    return jnp.concatenate([ref[2 * block : 2 * block + 1, :], ref[2 * block + 1 : 2 * block + 2, :]], axis=1)


def build_tables(cell_ref, offset_ref, weight_ref, mask_ref, count_ref, table_z, table_y, table_x, strength_ref):
    count = count_ref[0]
    for block in range(BLOCKS):
        lanes = pl.ds(block * BLOCK, BLOCK)

        def factors(axis):
            return cell_ref[axis : axis + 1, lanes], spline_weights(offset_ref[axis : axis + 1, lanes])

        def spread_out(cell, rows, parts):
            apart = lax.broadcasted_iota(jnp.int32, (rows, BLOCK), 0) - cell
            zero = jnp.zeros((rows, BLOCK), jnp.float32)
            before, at, after = apart == -1, apart == 0, apart == 1
            return [jnp.where(before, a, jnp.where(at, b, jnp.where(after, c, zero))) for a, b, c in parts]

        cell, parts = factors(2)
        terms = [two_terms(part) for part in parts]
        high, low = spread_out(
            cell,
            COLS,
            [[t[0].astype(jnp.float32) for t in terms], [t[1].astype(jnp.float32) for t in terms]],
        )
        table_z[0:COLS, lanes] = high.astype(jnp.bfloat16)
        table_z[COLS : 2 * COLS, lanes] = low.astype(jnp.bfloat16)
        cell, parts = factors(1)
        table_y[:, lanes] = spread_out(cell, ROWS, [parts])[0]
        cell, parts = factors(0)
        table_x[:, lanes] = spread_out(cell, 8, [parts])[0]
        alive = jnp.where(count > block, 1.0, 0.0)
        strength_ref[0:1, lanes] = (
            jnp.where(block_row(mask_ref, block) == 1, block_row(weight_ref, block), 0.0) * alive
        )


def screen(field, table_z, table_y, table_x, strength_ref, left_ref, spread_ref):
    high, low = two_terms(field)
    left_ref[0:CELLS, 0:COLS] = high
    left_ref[0:CELLS, COLS : 2 * COLS] = high
    left_ref[CELLS : 2 * CELLS, 0:COLS] = low
    left_ref[CELLS : 2 * CELLS, COLS : 2 * COLS] = low
    for block in range(BLOCKS):
        lanes = pl.ds(block * BLOCK, BLOCK)
        both = jnp.dot(left_ref[...], table_z[:, lanes], preferred_element_type=jnp.float32)
        sampled = (both[0:CELLS] + both[CELLS : 2 * CELLS]).reshape(PLANES, ROWS, BLOCK)
        along_y = table_y[:, lanes]
        along_x = table_x[:, lanes]
        total = jnp.zeros((8, BLOCK), jnp.float32)
        for plane in range(PLANES):
            summed = jnp.sum((sampled[plane] * along_y).reshape(ROWS // 8, 8, BLOCK), axis=0)
            total = total + summed * along_x[plane : plane + 1]
        values = jnp.sum(total, axis=0, keepdims=True) * strength_ref[0:1, lanes]
        for plane in range(PLANES):
            high, low = two_terms(along_y * (along_x[plane : plane + 1] * values))
            spread_ref[plane * ROWS : (plane + 1) * ROWS, lanes] = high
            spread_ref[CELLS + plane * ROWS : CELLS + (plane + 1) * ROWS, lanes] = low
    result = lax.dot_general(
        spread_ref[...], table_z[...], (((1,), (1,)), ((), ())), preferred_element_type=jnp.float32
    )
    result = result[0:CELLS] + result[CELLS : 2 * CELLS]
    return result[:, 0:COLS] + result[:, COLS : 2 * COLS]


def mass(values):
    return (66.0 / 120.0) * values[2] + (26.0 / 120.0) * (values[1] + values[3]) + (1.0 / 120.0) * (values[0] + values[4])


def stiff(values):
    return values[2] - (1.0 / 3.0) * (values[1] + values[3]) - (1.0 / 6.0) * (values[0] + values[4])


def stencil(field_ref, first, last, stiff_ref, mass_ref):
    planes = [field_ref[k] for k in range(PLANES + 4)]
    planes[0:2] = [jnp.where(first, 0.0, p) for p in planes[0:2]]
    planes[6:8] = [jnp.where(last, 0.0, p) for p in planes[6:8]]
    for k in range(PLANES):
        stiff_ref[k, EDGE : EDGE + ROWS, :] = stiff(planes[k : k + 5])
        mass_ref[k, EDGE : EDGE + ROWS, :] = mass(planes[k : k + 5])
    lane = lax.broadcasted_iota(jnp.int32, (ROWS, COLS), 1)

    def along_z(value):
        return [
            jnp.where(lane >= 2, pltpu.roll(value, 2, 1), 0.0),
            jnp.where(lane >= 1, pltpu.roll(value, 1, 1), 0.0),
            value,
            jnp.where(lane < COLS - 1, pltpu.roll(value, COLS - 1, 1), 0.0),
            jnp.where(lane < COLS - 2, pltpu.roll(value, COLS - 2, 1), 0.0),
        ]

    out = []
    for k in range(PLANES):
        stiff_x = [stiff_ref[k, EDGE - 2 + s : EDGE - 2 + s + ROWS, :] for s in range(5)]
        mass_x = [mass_ref[k, EDGE - 2 + s : EDGE - 2 + s + ROWS, :] for s in range(5)]
        out.append(mass(along_z(mass(stiff_x) + stiff(mass_x))) + stiff(along_z(mass(mass_x))))
    return out


def combine(tiles):
    largest = functools.reduce(jnp.maximum, [t[4:5] for t in tiles])
    total = jnp.zeros((8, COLS), jnp.float32)
    for t in tiles:
        ratio = t[4:5] / largest
        total = total + t * (ratio * ratio)
    row = lax.broadcasted_iota(jnp.int32, (8, COLS), 0)
    return jnp.where(row == 4, largest, total)


def kernel(
    right_ref, guess_ref, cell_ref, offset_ref, weight_ref, mask_ref, count_ref,
    out_field, out_residual,
    guess, residual, image, second, stiff_ref, mass_ref,
    table_z, table_y, table_x, strength_ref, left_ref, spread_ref,
    sums, arrived_a, arrived_b,
    halo_send, halo_recv, sum_send, sum_recv,
):
    here = coordinates()
    device = lax.axis_index("bricks") * 4 + lax.axis_index("pts")
    before, after = (device + 255) % 256, (device + 1) % 256
    left, right = (before // 4, before % 4), (after // 4, after % 4)
    peers = [stage_peers(here, axes) for axes in STAGES]

    barrier = pltpu.get_barrier_semaphore()
    greeted = [left, right] + [p for stage in peers for p in stage]
    for peer in greeted:
        pl.semaphore_signal(barrier, inc=1, device_id=peer, device_id_type=MESH)

    guess[2:6] = guess_ref[...]
    for ref in (stiff_ref, mass_ref):
        ref[:, 0:EDGE, :] = jnp.zeros((PLANES, EDGE, COLS), jnp.float32)
        ref[:, EDGE + ROWS : 2 * EDGE + ROWS, :] = jnp.zeros((PLANES, EDGE, COLS), jnp.float32)
    build_tables(cell_ref, offset_ref, weight_ref, mask_ref, count_ref, table_z, table_y, table_x, strength_ref)
    tables = (table_z, table_y, table_x, strength_ref, left_ref, spread_ref)

    pl.semaphore_wait(barrier, len(greeted))

    def exchange(field, turn):
        copies = []
        for side, (source, target, to) in enumerate(((2, 6, left), (4, 0, right))):
            copy = pltpu.make_async_remote_copy(
                src_ref=field.at[pl.ds(source, 2)],
                dst_ref=field.at[pl.ds(target, 2)],
                send_sem=halo_send.at[turn, side],
                recv_sem=halo_recv.at[turn, side],
                device_id=to,
                device_id_type=MESH,
            )
            copy.start()
            copies.append(copy)
        return copies

    def operate(field, turn):
        copies = exchange(field, turn)
        screened = screen(field[2:6].reshape(CELLS, COLS), *tables).reshape(PLANES, ROWS, COLS)
        second[...] = screened
        for copy in copies:
            copy.wait_recv()
        smooth = stencil(field, device == 0, device == 255, stiff_ref, mass_ref)
        return copies, [smooth[k] + second[k] for k in range(PLANES)]

    started = []
    copies, product = operate(guess, 0)
    started += copies
    for k in range(PLANES):
        residual[2 + k] = right_ref[k] - product[k]
    copies, product = operate(residual, 1)
    started += copies
    for k in range(PLANES):
        image[2 + k] = product[k]
    copies, product = operate(image, 2)
    started += copies
    for k in range(PLANES):
        second[k] = product[k]

    def fold(value):
        return value.reshape(CELLS // 8, 8, COLS)

    r0 = fold(residual[2:6])
    scale = jnp.max(jnp.max(jnp.abs(r0), axis=0), axis=0, keepdims=True)
    scale = jnp.maximum(scale, 1e-30)
    inverse = 1.0 / scale
    r0 = r0 * inverse
    w = fold(image[2:6]) * inverse
    u = fold(second[...]) * inverse
    row = lax.broadcasted_iota(jnp.int32, (8, COLS), 0)
    tile = jnp.where(row == 4, scale, 0.0)
    for k, (a, b) in enumerate(((r0, r0), (r0, w), (w, w), (w, u))):
        moment = jnp.sum(jnp.sum(a * b, axis=0), axis=0, keepdims=True)
        tile = jnp.where(row == k, moment, tile)

    for turn, arrived in enumerate((arrived_a, arrived_b)):
        sums[turn] = tile
        for slot, peer in enumerate(peers[turn]):
            copy = pltpu.make_async_remote_copy(
                src_ref=sums.at[turn],
                dst_ref=arrived.at[slot],
                send_sem=sum_send.at[turn],
                recv_sem=sum_recv.at[turn],
                device_id=peer,
                device_id_type=MESH,
            )
            copy.start()
        pltpu.make_async_copy(arrived, arrived, sum_recv.at[turn]).wait()
        tile = combine([tile] + [arrived[slot] for slot in range(len(peers[turn]))])

    top = tile[4:5]
    ratio = top / jnp.max(top, axis=1, keepdims=True)
    moments = jnp.sum(tile * (ratio * ratio), axis=1, keepdims=True)
    m0, m1, m2, m3 = (moments[k : k + 1] for k in range(4))
    a0 = m0 / m1
    g = a0 * (m2 / m1)
    a1 = (g - 1.0) * m1 / (a0 * m3 - g * m2)
    c1 = a0 + a1 * g
    c2 = a1 * a0
    for k in range(PLANES):
        out_field[k] = guess[2 + k] + c1 * residual[2 + k] - c2 * image[2 + k]
        out_residual[k] = residual[2 + k] - c1 * image[2 + k] + c2 * second[k]

    for copy in started:
        copy.wait_send()
    for turn, arrived in enumerate((arrived_a, arrived_b)):
        pltpu.make_async_copy(arrived, arrived, sum_send.at[turn]).wait()


def body(right_side, initial_guess, point_cell, point_offset, point_weight, point_mask, block_count):
    slab = jax.ShapeDtypeStruct((PLANES, ROWS, COLS), jnp.float32)
    vmem = pl.BlockSpec(memory_space=pltpu.VMEM)
    groups = []
    for axes in STAGES:
        size = 1
        for axis in axes:
            size *= SIZES[axis]
        groups.append(size - 1)
    return pl.pallas_call(
        kernel,
        out_shape=(slab, slab),
        in_specs=[vmem] * 6 + [pl.BlockSpec(memory_space=pltpu.SMEM)],
        out_specs=(vmem, vmem),
        scratch_shapes=[
            pltpu.VMEM((PLANES + 4, ROWS, COLS), jnp.float32),
            pltpu.VMEM((PLANES + 4, ROWS, COLS), jnp.float32),
            pltpu.VMEM((PLANES + 4, ROWS, COLS), jnp.float32),
            pltpu.VMEM((PLANES, ROWS, COLS), jnp.float32),
            pltpu.VMEM((PLANES, ROWS + 2 * EDGE, COLS), jnp.float32),
            pltpu.VMEM((PLANES, ROWS + 2 * EDGE, COLS), jnp.float32),
            pltpu.VMEM((2 * COLS, POINTS), jnp.bfloat16),
            pltpu.VMEM((ROWS, POINTS), jnp.float32),
            pltpu.VMEM((8, POINTS), jnp.float32),
            pltpu.VMEM((8, POINTS), jnp.float32),
            pltpu.VMEM((2 * CELLS, 2 * COLS), jnp.bfloat16),
            pltpu.VMEM((2 * CELLS, POINTS), jnp.bfloat16),
            pltpu.VMEM((2, 8, COLS), jnp.float32),
            pltpu.VMEM((groups[0], 8, COLS), jnp.float32),
            pltpu.VMEM((groups[1], 8, COLS), jnp.float32),
            pltpu.SemaphoreType.DMA((3, 2)),
            pltpu.SemaphoreType.DMA((3, 2)),
            pltpu.SemaphoreType.DMA((2,)),
            pltpu.SemaphoreType.DMA((2,)),
        ],
        compiler_params=pltpu.CompilerParams(
            collective_id=0, has_side_effects=True, vmem_limit_bytes=32 * 1024 * 1024
        ),
        cost_estimate=pl.CostEstimate(flops=3_000_000_000, bytes_accessed=700_000, transcendentals=0),
    )(
        right_side, initial_guess, point_cell, point_offset,
        point_weight.reshape(16, 128), point_mask.reshape(16, 128), block_count,
    )


def solution(mesh):
    placed = (
        P(("bricks", "pts"), None, None),
        P(("bricks", "pts"), None, None),
        P(None, ("bricks", "pts")),
        P(None, ("bricks", "pts")),
        P(("bricks", "pts")),
        P(("bricks", "pts")),
        P(("bricks", "pts")),
    )
    return jax.shard_map(
        body,
        mesh=mesh,
        in_specs=placed,
        out_specs=(P(("bricks", "pts"), None, None), P(("bricks", "pts"), None, None)),
        check_vma=False,
    )
```

```python
import functools

import jax
import jax.numpy as jnp
from jax import lax
from jax.experimental import pallas as pl
from jax.experimental.pallas import tpu as pltpu
from jax.sharding import PartitionSpec as P

MESH = pl.DeviceIdType.MESH

PLANES = 4
ROWS = 64
COLS = 128
CELLS = PLANES * ROWS
BLOCK = 256
BLOCKS = 8
POINTS = BLOCK * BLOCKS
EDGE = 8

SIZES = {"x": 4, "y": 4, "z": 8, "core": 2}
STAGES = (("x", "y", "core"), ("z",))


def spline_weights(offset):
    return (0.5 * (0.5 - offset) ** 2, 0.75 - offset * offset, 0.5 * (0.5 + offset) ** 2)


def coordinates():
    brick = lax.axis_index("bricks")
    return {
        "x": lax.axis_index("pts"),
        "y": brick // 16,
        "z": (brick // 2) % 8,
        "core": brick % 2,
    }


def device_of(place):
    return ((place["y"] * 8 + place["z"]) * 2 + place["core"], place["x"])


def stage_peers(here, axes):
    steps = [{}]
    for axis in axes:
        steps = [dict(step, **{axis: k}) for step in steps for k in range(SIZES[axis])]
    peers = []
    for step in steps[1:]:
        place = dict(here)
        for axis, k in step.items():
            if k:
                place[axis] = (here[axis] + k) % SIZES[axis]
        peers.append(device_of(place))
    return peers


def two_terms(value):
    high = value.astype(jnp.bfloat16)
    low = (value - high.astype(jnp.float32)).astype(jnp.bfloat16)
    return high, low


def block_row(ref, block):
    return jnp.concatenate([ref[2 * block : 2 * block + 1, :], ref[2 * block + 1 : 2 * block + 2, :]], axis=1)


def build_tables(cell_ref, offset_ref, weight_ref, mask_ref, count_ref, table_z, table_y, table_x, strength_ref):
    count = count_ref[0]
    for block in range(BLOCKS):
        lanes = pl.ds(block * BLOCK, BLOCK)

        def factors(axis):
            return cell_ref[axis : axis + 1, lanes], spline_weights(offset_ref[axis : axis + 1, lanes])

        def spread_out(cell, rows, parts):
            apart = lax.broadcasted_iota(jnp.int32, (rows, BLOCK), 0) - cell
            zero = jnp.zeros((rows, BLOCK), jnp.float32)
            before, at, after = apart == -1, apart == 0, apart == 1
            return [jnp.where(before, a, jnp.where(at, b, jnp.where(after, c, zero))) for a, b, c in parts]

        cell, parts = factors(2)
        terms = [two_terms(part) for part in parts]
        high, low = spread_out(
            cell,
            COLS,
            [[t[0].astype(jnp.float32) for t in terms], [t[1].astype(jnp.float32) for t in terms]],
        )
        table_z[0:COLS, lanes] = high.astype(jnp.bfloat16)
        table_z[COLS : 2 * COLS, lanes] = low.astype(jnp.bfloat16)
        cell, parts = factors(1)
        table_y[:, lanes] = spread_out(cell, ROWS, [parts])[0]
        cell, parts = factors(0)
        table_x[:, lanes] = spread_out(cell, 8, [parts])[0]
        alive = jnp.where(count > block, 1.0, 0.0)
        strength_ref[0:1, lanes] = (
            jnp.where(block_row(mask_ref, block) == 1, block_row(weight_ref, block), 0.0) * alive
        )


def screen(field, table_z, table_y, table_x, strength_ref, left_ref, spread_ref):
    high, low = two_terms(field)
    left_ref[0:CELLS, 0:COLS] = high
    left_ref[0:CELLS, COLS : 2 * COLS] = high
    left_ref[CELLS : 2 * CELLS, 0:COLS] = low
    left_ref[CELLS : 2 * CELLS, COLS : 2 * COLS] = low
    for block in range(BLOCKS):
        lanes = pl.ds(block * BLOCK, BLOCK)
        both = jnp.dot(left_ref[...], table_z[:, lanes], preferred_element_type=jnp.float32)
        sampled = (both[0:CELLS] + both[CELLS : 2 * CELLS]).reshape(PLANES, ROWS, BLOCK)
        along_y = table_y[:, lanes]
        along_x = table_x[:, lanes]
        total = jnp.zeros((8, BLOCK), jnp.float32)
        for plane in range(PLANES):
            summed = jnp.sum((sampled[plane] * along_y).reshape(ROWS // 8, 8, BLOCK), axis=0)
            total = total + summed * along_x[plane : plane + 1]
        values = jnp.sum(total, axis=0, keepdims=True) * strength_ref[0:1, lanes]
        for plane in range(PLANES):
            high, low = two_terms(along_y * (along_x[plane : plane + 1] * values))
            spread_ref[plane * ROWS : (plane + 1) * ROWS, lanes] = high
            spread_ref[CELLS + plane * ROWS : CELLS + (plane + 1) * ROWS, lanes] = low
    result = lax.dot_general(
        spread_ref[...], table_z[...], (((1,), (1,)), ((), ())), preferred_element_type=jnp.float32
    )
    result = result[0:CELLS] + result[CELLS : 2 * CELLS]
    return result[:, 0:COLS] + result[:, COLS : 2 * COLS]


def mass(values):
    return (66.0 / 120.0) * values[2] + (26.0 / 120.0) * (values[1] + values[3]) + (1.0 / 120.0) * (values[0] + values[4])


def stiff(values):
    return values[2] - (1.0 / 3.0) * (values[1] + values[3]) - (1.0 / 6.0) * (values[0] + values[4])


def stencil(planes, stiff_ref, mass_ref):
    count = len(planes) - 4
    for k in range(count):
        stiff_ref[k, EDGE : EDGE + ROWS, :] = stiff(planes[k : k + 5])
        mass_ref[k, EDGE : EDGE + ROWS, :] = mass(planes[k : k + 5])
    lane = lax.broadcasted_iota(jnp.int32, (ROWS, COLS), 1)

    def along_z(value):
        return [
            jnp.where(lane >= 2, pltpu.roll(value, 2, 1), 0.0),
            jnp.where(lane >= 1, pltpu.roll(value, 1, 1), 0.0),
            value,
            jnp.where(lane < COLS - 1, pltpu.roll(value, COLS - 1, 1), 0.0),
            jnp.where(lane < COLS - 2, pltpu.roll(value, COLS - 2, 1), 0.0),
        ]

    out = []
    for k in range(count):
        stiff_x = [stiff_ref[k, EDGE - 2 + s : EDGE - 2 + s + ROWS, :] for s in range(5)]
        mass_x = [mass_ref[k, EDGE - 2 + s : EDGE - 2 + s + ROWS, :] for s in range(5)]
        out.append(mass(along_z(mass(stiff_x) + stiff(mass_x))) + stiff(along_z(mass(mass_x))))
    return out


def packed(moments, scale):
    lane = lax.broadcasted_iota(jnp.int32, (1, COLS), 1)
    row = jnp.broadcast_to(scale, (1, COLS))
    for k, moment in enumerate(moments):
        for shift in (64, 32, 16):
            moment = moment + pltpu.roll(moment, shift, 1)
        row = jnp.where(lane // 16 == k, moment, row)
    return row


def combine(rows):
    lane = lax.broadcasted_iota(jnp.int32, rows.shape, 1)
    scales = jnp.max(jnp.where(lane >= 64, rows, 0.0), axis=1, keepdims=True)
    largest = jnp.max(scales, axis=0, keepdims=True)
    ratio = scales / largest
    total = jnp.sum(rows * (ratio * ratio), axis=0, keepdims=True)
    return jnp.where(lane[0:1] >= 64, largest, total)


def kernel(
    right_in, guess_in, cell_in, offset_in, weight_in, mask_in, count_ref,
    out_field, out_residual,
    right_ref, cell_ref, offset_ref, weight_ref, mask_ref,
    guess, known, residual, image, second, stiff_ref, mass_ref,
    table_z, table_y, table_x, strength_ref, left_ref, spread_ref,
    sums, arrived_a, arrived_b,
    load_sem, halo_send, halo_recv, sum_send, sum_recv,
):
    loads = [
        pltpu.make_async_copy(source, target, load_sem.at[k])
        for k, (source, target) in enumerate((
            (cell_in, cell_ref),
            (offset_in, offset_ref),
            (weight_in, weight_ref),
            (mask_in, mask_ref),
            (guess_in, guess.at[pl.ds(4, PLANES)]),
            (right_in, right_ref),
        ))
    ]
    for load in loads:
        load.start()

    here = coordinates()
    device = lax.axis_index("bricks") * 4 + lax.axis_index("pts")
    before, after = (device + 255) % 256, (device + 1) % 256
    left, right = (before // 4, before % 4), (after // 4, after % 4)
    peers = [stage_peers(here, axes) for axes in STAGES]

    barrier = pltpu.get_barrier_semaphore()
    greeted = [left, right] + [p for stage in peers for p in stage]
    for peer in greeted:
        pl.semaphore_signal(barrier, inc=1, device_id=peer, device_id_type=MESH)

    first, last = device == 0, device == 255
    for ref in (stiff_ref, mass_ref):
        ref[:, 0:EDGE, :] = jnp.zeros((PLANES, EDGE, COLS), jnp.float32)
        ref[:, EDGE + ROWS : 2 * EDGE + ROWS, :] = jnp.zeros((PLANES, EDGE, COLS), jnp.float32)
    for load in loads[0:4]:
        load.wait()
    build_tables(cell_ref, offset_ref, weight_ref, mask_ref, count_ref, table_z, table_y, table_x, strength_ref)
    tables = (table_z, table_y, table_x, strength_ref, left_ref, spread_ref)

    loads[4].wait()
    pl.semaphore_wait(barrier, len(greeted))
    started = []

    def send(field, turn, moves):
        copies = []
        for side, (source, target) in enumerate(moves):
            copy = pltpu.make_async_remote_copy(
                src_ref=field.at[pl.ds(source, 2)],
                dst_ref=field.at[pl.ds(target, 2)],
                send_sem=halo_send.at[turn, side],
                recv_sem=halo_recv.at[turn, side],
                device_id=(left, right)[side],
                device_id_type=MESH,
            )
            copy.start()
            copies.append(copy)
        started.extend(copies)
        return copies

    def landed(copies):
        for copy in copies:
            copy.wait_recv()

    def screened(field):
        return screen(field.reshape(CELLS, COLS), *tables).reshape(PLANES, ROWS, COLS)

    def outside(planes, side):
        return [jnp.where(side, 0.0, p) for p in planes]

    near = send(guess, 0, ((4, 8), (6, 2)))
    far = send(guess, 1, ((6, 10), (4, 0)))
    value = screened(guess[4:8])
    loads[5].wait()
    known[2:6] = right_ref[...] - value
    edge = send(known, 2, ((2, 6), (4, 0)))

    landed(near)
    planes = outside([guess[k] for k in (2, 3)], first) + [guess[k] for k in range(4, 8)]
    planes = planes + outside([guess[k] for k in (8, 9)], last)
    smooth = stencil(planes, stiff_ref, mass_ref)
    for k in range(PLANES):
        residual[2 + k] = known[2 + k] - smooth[k]
    second[...] = screened(residual[2:6])

    landed(far)
    landed(edge)
    smooth = stencil([guess[k] for k in range(0, 6)], stiff_ref, mass_ref)
    for k in range(2):
        residual[k] = jnp.where(first, 0.0, known[k] - smooth[k])
    smooth = stencil([guess[k] for k in range(6, 12)], stiff_ref, mass_ref)
    for k in range(2):
        residual[6 + k] = jnp.where(last, 0.0, known[6 + k] - smooth[k])
    smooth = stencil([residual[k] for k in range(8)], stiff_ref, mass_ref)
    for k in range(PLANES):
        image[2 + k] = smooth[k] + second[k]
    edge = send(image, 3, ((2, 6), (4, 0)))

    value = screened(image[2:6])
    second[...] = value
    landed(edge)
    planes = outside([image[k] for k in (0, 1)], first) + [image[k] for k in range(2, 6)]
    planes = planes + outside([image[k] for k in (6, 7)], last)
    smooth = stencil(planes, stiff_ref, mass_ref)
    for k in range(PLANES):
        second[k] = second[k] + smooth[k]

    def fold(value):
        return value.reshape(CELLS // 8, 8, COLS)

    r0 = fold(residual[2:6])
    scale = jnp.max(jnp.max(jnp.abs(r0), axis=0), axis=0, keepdims=True)
    scale = jnp.maximum(jnp.max(scale, axis=1, keepdims=True), 1e-30)
    inverse = 1.0 / scale
    r0 = r0 * inverse
    w = fold(image[2:6]) * inverse
    u = fold(second[...]) * inverse
    moments = [
        jnp.sum(jnp.sum(a * b, axis=0), axis=0, keepdims=True) for a, b in ((r0, r0), (r0, w), (w, w), (w, u))
    ]
    row = packed(moments, scale)

    for turn, arrived in enumerate((arrived_a, arrived_b)):
        count = len(peers[turn])
        sums[turn] = row
        arrived[count : count + 1, :] = row
        for slot, peer in enumerate(peers[turn]):
            pltpu.make_async_remote_copy(
                src_ref=sums.at[turn],
                dst_ref=arrived.at[pl.ds(slot, 1)],
                send_sem=sum_send.at[turn],
                recv_sem=sum_recv.at[turn],
                device_id=peer,
                device_id_type=MESH,
            ).start()
        whole = arrived.at[pl.ds(0, count)]
        pltpu.make_async_copy(whole, whole, sum_recv.at[turn]).wait()
        row = combine(arrived[...])

    lane = lax.broadcasted_iota(jnp.int32, (1, COLS), 1)
    m0, m1, m2, m3 = (
        jnp.sum(jnp.where(lane // 16 == k, row, 0.0), axis=1, keepdims=True) for k in range(4)
    )
    a0 = m0 / m1
    g = a0 * (m2 / m1)
    a1 = (g - 1.0) * m1 / (a0 * m3 - g * m2)
    c1 = a0 + a1 * g
    c2 = a1 * a0
    for k in range(PLANES):
        out_field[k] = guess[4 + k] + c1 * residual[2 + k] - c2 * image[2 + k]
        out_residual[k] = residual[2 + k] - c1 * image[2 + k] + c2 * second[k]

    for copy in started:
        copy.wait_send()
    for turn, arrived in enumerate((arrived_a, arrived_b)):
        whole = arrived.at[pl.ds(0, len(peers[turn]))]
        pltpu.make_async_copy(whole, whole, sum_send.at[turn]).wait()


def body(right_side, initial_guess, point_cell, point_offset, point_weight, point_mask, block_count):
    slab = jax.ShapeDtypeStruct((PLANES, ROWS, COLS), jnp.float32)
    vmem = pl.BlockSpec(memory_space=pltpu.VMEM)
    groups = []
    for axes in STAGES:
        size = 1
        for axis in axes:
            size *= SIZES[axis]
        groups.append(size)
    return pl.pallas_call(
        kernel,
        out_shape=(slab, slab),
        in_specs=[pl.BlockSpec(memory_space=pltpu.HBM)] * 6 + [pl.BlockSpec(memory_space=pltpu.SMEM)],
        out_specs=(vmem, vmem),
        scratch_shapes=[
            pltpu.VMEM((PLANES, ROWS, COLS), jnp.float32),
            pltpu.VMEM((3, POINTS), jnp.int32),
            pltpu.VMEM((3, POINTS), jnp.float32),
            pltpu.VMEM((POINTS // COLS, COLS), jnp.float32),
            pltpu.VMEM((POINTS // COLS, COLS), jnp.int32),
            pltpu.VMEM((PLANES + 8, ROWS, COLS), jnp.float32),
            pltpu.VMEM((PLANES + 4, ROWS, COLS), jnp.float32),
            pltpu.VMEM((PLANES + 4, ROWS, COLS), jnp.float32),
            pltpu.VMEM((PLANES + 4, ROWS, COLS), jnp.float32),
            pltpu.VMEM((PLANES, ROWS, COLS), jnp.float32),
            pltpu.VMEM((PLANES, ROWS + 2 * EDGE, COLS), jnp.float32),
            pltpu.VMEM((PLANES, ROWS + 2 * EDGE, COLS), jnp.float32),
            pltpu.VMEM((2 * COLS, POINTS), jnp.bfloat16),
            pltpu.VMEM((ROWS, POINTS), jnp.float32),
            pltpu.VMEM((8, POINTS), jnp.float32),
            pltpu.VMEM((8, POINTS), jnp.float32),
            pltpu.VMEM((2 * CELLS, 2 * COLS), jnp.bfloat16),
            pltpu.VMEM((2 * CELLS, POINTS), jnp.bfloat16),
            pltpu.VMEM((2, 1, COLS), jnp.float32),
            pltpu.VMEM((groups[0], COLS), jnp.float32),
            pltpu.VMEM((groups[1], COLS), jnp.float32),
            pltpu.SemaphoreType.DMA((6,)),
            pltpu.SemaphoreType.DMA((4, 2)),
            pltpu.SemaphoreType.DMA((4, 2)),
            pltpu.SemaphoreType.DMA((2,)),
            pltpu.SemaphoreType.DMA((2,)),
        ],
        compiler_params=pltpu.CompilerParams(
            collective_id=0, has_side_effects=True, vmem_limit_bytes=56 * 1024 * 1024
        ),
        cost_estimate=pl.CostEstimate(flops=3_000_000_000, bytes_accessed=700_000, transcendentals=0),
    )(
        right_side, initial_guess, point_cell, point_offset,
        point_weight.reshape(POINTS // COLS, COLS), point_mask.reshape(POINTS // COLS, COLS), block_count,
    )


def solution(mesh):
    placed = (
        P(("bricks", "pts"), None, None),
        P(("bricks", "pts"), None, None),
        P(None, ("bricks", "pts")),
        P(None, ("bricks", "pts")),
        P(("bricks", "pts")),
        P(("bricks", "pts")),
        P(("bricks", "pts")),
    )
    return jax.shard_map(
        body,
        mesh=mesh,
        in_specs=placed,
        out_specs=(P(("bricks", "pts"), None, None), P(("bricks", "pts"), None, None)),
        check_vma=False,
    )
```

```python
import functools

import jax
import jax.numpy as jnp
from jax import lax
from jax.experimental import pallas as pl
from jax.experimental.pallas import tpu as pltpu
from jax.sharding import PartitionSpec as P

MESH = pl.DeviceIdType.MESH

PLANES = 4
ROWS = 64
COLS = 128
CELLS = PLANES * ROWS
BLOCK = 256
BLOCKS = 8
POINTS = BLOCK * BLOCKS
EDGE = 8

SIZES = {"x": 4, "y": 4, "z": 8, "core": 2}
STAGES = (("x", "y", "core"), ("z",))


def spline_weights(offset):
    return (0.5 * (0.5 - offset) ** 2, 0.75 - offset * offset, 0.5 * (0.5 + offset) ** 2)


def coordinates():
    brick = lax.axis_index("bricks")
    return {
        "x": lax.axis_index("pts"),
        "y": brick // 16,
        "z": (brick // 2) % 8,
        "core": brick % 2,
    }


def device_of(place):
    return ((place["y"] * 8 + place["z"]) * 2 + place["core"], place["x"])


def stage_peers(here, axes):
    steps = [{}]
    for axis in axes:
        steps = [dict(step, **{axis: k}) for step in steps for k in range(SIZES[axis])]
    peers = []
    for step in steps[1:]:
        place = dict(here)
        for axis, k in step.items():
            if k:
                place[axis] = (here[axis] + k) % SIZES[axis]
        peers.append(device_of(place))
    return peers


def two_terms(value):
    high = value.astype(jnp.bfloat16)
    low = (value - high.astype(jnp.float32)).astype(jnp.bfloat16)
    return high, low


def block_row(ref, block):
    return jnp.concatenate([ref[2 * block : 2 * block + 1, :], ref[2 * block + 1 : 2 * block + 2, :]], axis=1)


def build_tables(cell_ref, offset_ref, weight_ref, mask_ref, count_ref, table_z, table_y, table_x, strength_ref):
    count = count_ref[0]
    for block in range(BLOCKS):
        lanes = pl.ds(block * BLOCK, BLOCK)

        def factors(axis):
            return cell_ref[axis : axis + 1, lanes], spline_weights(offset_ref[axis : axis + 1, lanes])

        def spread_out(cell, rows, parts):
            apart = lax.broadcasted_iota(jnp.int32, (rows, BLOCK), 0) - cell
            zero = jnp.zeros((rows, BLOCK), jnp.float32)
            before, at, after = apart == -1, apart == 0, apart == 1
            return [jnp.where(before, a, jnp.where(at, b, jnp.where(after, c, zero))) for a, b, c in parts]

        cell, parts = factors(2)
        terms = [two_terms(part) for part in parts]
        high, low = spread_out(
            cell,
            COLS,
            [[t[0].astype(jnp.float32) for t in terms], [t[1].astype(jnp.float32) for t in terms]],
        )
        table_z[0:COLS, lanes] = high.astype(jnp.bfloat16)
        table_z[COLS : 2 * COLS, lanes] = low.astype(jnp.bfloat16)
        cell, parts = factors(1)
        table_y[:, lanes] = spread_out(cell, ROWS, [parts])[0]
        cell, parts = factors(0)
        table_x[:, lanes] = spread_out(cell, 8, [parts])[0]
        alive = jnp.where(count > block, 1.0, 0.0)
        strength_ref[0:1, lanes] = (
            jnp.where(block_row(mask_ref, block) == 1, block_row(weight_ref, block), 0.0) * alive
        )


def screen(field, table_z, table_y, table_x, strength_ref, left_ref, spread_ref):
    high, low = two_terms(field)
    left_ref[0:CELLS, 0:COLS] = high
    left_ref[0:CELLS, COLS : 2 * COLS] = high
    left_ref[CELLS : 2 * CELLS, 0:COLS] = low
    left_ref[CELLS : 2 * CELLS, COLS : 2 * COLS] = low
    for block in range(BLOCKS):
        lanes = pl.ds(block * BLOCK, BLOCK)
        both = jnp.dot(left_ref[...], table_z[:, lanes], preferred_element_type=jnp.float32)
        sampled = (both[0:CELLS] + both[CELLS : 2 * CELLS]).reshape(PLANES, ROWS, BLOCK)
        along_y = table_y[:, lanes]
        along_x = table_x[:, lanes]
        total = jnp.zeros((8, BLOCK), jnp.float32)
        for plane in range(PLANES):
            summed = jnp.sum((sampled[plane] * along_y).reshape(ROWS // 8, 8, BLOCK), axis=0)
            total = total + summed * along_x[plane : plane + 1]
        values = jnp.sum(total, axis=0, keepdims=True) * strength_ref[0:1, lanes]
        for plane in range(PLANES):
            high, low = two_terms(along_y * (along_x[plane : plane + 1] * values))
            spread_ref[plane * ROWS : (plane + 1) * ROWS, lanes] = high
            spread_ref[CELLS + plane * ROWS : CELLS + (plane + 1) * ROWS, lanes] = low
    result = lax.dot_general(
        spread_ref[...], table_z[...], (((1,), (1,)), ((), ())), preferred_element_type=jnp.float32
    )
    result = result[0:CELLS] + result[CELLS : 2 * CELLS]
    return result[:, 0:COLS] + result[:, COLS : 2 * COLS]


def mass(values):
    return (66.0 / 120.0) * values[2] + (26.0 / 120.0) * (values[1] + values[3]) + (1.0 / 120.0) * (values[0] + values[4])


def stiff(values):
    return values[2] - (1.0 / 3.0) * (values[1] + values[3]) - (1.0 / 6.0) * (values[0] + values[4])


def stencil(planes, stiff_ref, mass_ref):
    count = len(planes) - 4
    for k in range(count):
        stiff_ref[k, EDGE : EDGE + ROWS, :] = stiff(planes[k : k + 5])
        mass_ref[k, EDGE : EDGE + ROWS, :] = mass(planes[k : k + 5])
    lane = lax.broadcasted_iota(jnp.int32, (ROWS, COLS), 1)

    def along_z(value):
        return [
            jnp.where(lane >= 2, pltpu.roll(value, 2, 1), 0.0),
            jnp.where(lane >= 1, pltpu.roll(value, 1, 1), 0.0),
            value,
            jnp.where(lane < COLS - 1, pltpu.roll(value, COLS - 1, 1), 0.0),
            jnp.where(lane < COLS - 2, pltpu.roll(value, COLS - 2, 1), 0.0),
        ]

    out = []
    for k in range(count):
        stiff_x = [stiff_ref[k, EDGE - 2 + s : EDGE - 2 + s + ROWS, :] for s in range(5)]
        mass_x = [mass_ref[k, EDGE - 2 + s : EDGE - 2 + s + ROWS, :] for s in range(5)]
        out.append(mass(along_z(mass(stiff_x) + stiff(mass_x))) + stiff(along_z(mass(mass_x))))
    return out


def packed(moments, scale):
    lane = lax.broadcasted_iota(jnp.int32, (1, COLS), 1)
    row = jnp.broadcast_to(scale, (1, COLS))
    for k, moment in enumerate(moments):
        for shift in (64, 32, 16):
            moment = moment + pltpu.roll(moment, shift, 1)
        row = jnp.where(lane // 16 == k, moment, row)
    return row


def combine(rows):
    lane = lax.broadcasted_iota(jnp.int32, rows.shape, 1)
    scales = jnp.max(jnp.where(lane >= 64, rows, 0.0), axis=1, keepdims=True)
    largest = jnp.max(scales, axis=0, keepdims=True)
    ratio = scales / largest
    total = jnp.sum(rows * (ratio * ratio), axis=0, keepdims=True)
    return jnp.where(lane[0:1] >= 64, largest, total)


def kernel(
    right_in, guess_in, cell_in, offset_in, weight_in, mask_in, count_ref,
    out_residual, out_image, out_second, out_factor,
    right_ref, cell_ref, offset_ref, weight_ref, mask_ref,
    guess, known, residual, image, second, stiff_ref, mass_ref,
    table_z, table_y, table_x, strength_ref, left_ref, spread_ref,
    load_sem, halo_send, halo_recv, sum_send, sum_recv, sums, *arrivals,
):
    loads = [
        pltpu.make_async_copy(source, target, load_sem.at[k])
        for k, (source, target) in enumerate((
            (cell_in, cell_ref),
            (offset_in, offset_ref),
            (weight_in, weight_ref),
            (mask_in, mask_ref),
            (guess_in, guess.at[pl.ds(4, PLANES)]),
            (right_in, right_ref),
        ))
    ]
    for load in loads:
        load.start()

    here = coordinates()
    device = lax.axis_index("bricks") * 4 + lax.axis_index("pts")
    before, after = (device + 255) % 256, (device + 1) % 256
    left, right = (before // 4, before % 4), (after // 4, after % 4)
    peers = [stage_peers(here, axes) for axes in STAGES]

    barrier = pltpu.get_barrier_semaphore()
    greeted = [left, right] + [p for stage in peers for p in stage]
    for peer in greeted:
        pl.semaphore_signal(barrier, inc=1, device_id=peer, device_id_type=MESH)

    first, last = device == 0, device == 255
    for ref in (stiff_ref, mass_ref):
        ref[:, 0:EDGE, :] = jnp.zeros((PLANES, EDGE, COLS), jnp.float32)
        ref[:, EDGE + ROWS : 2 * EDGE + ROWS, :] = jnp.zeros((PLANES, EDGE, COLS), jnp.float32)
    for load in loads[0:4]:
        load.wait()
    build_tables(cell_ref, offset_ref, weight_ref, mask_ref, count_ref, table_z, table_y, table_x, strength_ref)
    tables = (table_z, table_y, table_x, strength_ref, left_ref, spread_ref)

    loads[4].wait()
    pl.semaphore_wait(barrier, len(greeted))
    started = []

    def send(field, turn, moves):
        copies = []
        for side, (source, target) in enumerate(moves):
            copy = pltpu.make_async_remote_copy(
                src_ref=field.at[pl.ds(source, 2)],
                dst_ref=field.at[pl.ds(target, 2)],
                send_sem=halo_send.at[turn, side],
                recv_sem=halo_recv.at[turn, side],
                device_id=(left, right)[side],
                device_id_type=MESH,
            )
            copy.start()
            copies.append(copy)
        started.extend(copies)
        return copies

    def landed(copies):
        for copy in copies:
            copy.wait_recv()

    def screened(field):
        return screen(field.reshape(CELLS, COLS), *tables).reshape(PLANES, ROWS, COLS)

    def outside(planes, side):
        return [jnp.where(side, 0.0, p) for p in planes]

    near = send(guess, 0, ((4, 8), (6, 2)))
    far = send(guess, 1, ((6, 10), (4, 0)))
    value = screened(guess[4:8])
    loads[5].wait()
    known[2:6] = right_ref[...] - value
    edge = send(known, 2, ((2, 6), (4, 0)))

    landed(near)
    planes = outside([guess[k] for k in (2, 3)], first) + [guess[k] for k in range(4, 8)]
    planes = planes + outside([guess[k] for k in (8, 9)], last)
    smooth = stencil(planes, stiff_ref, mass_ref)
    for k in range(PLANES):
        residual[2 + k] = known[2 + k] - smooth[k]
    second[...] = screened(residual[2:6])

    landed(far)
    landed(edge)
    smooth = stencil([guess[k] for k in range(0, 6)], stiff_ref, mass_ref)
    for k in range(2):
        residual[k] = jnp.where(first, 0.0, known[k] - smooth[k])
    smooth = stencil([guess[k] for k in range(6, 12)], stiff_ref, mass_ref)
    for k in range(2):
        residual[6 + k] = jnp.where(last, 0.0, known[6 + k] - smooth[k])
    smooth = stencil([residual[k] for k in range(8)], stiff_ref, mass_ref)
    for k in range(PLANES):
        image[2 + k] = smooth[k] + second[k]
    edge = send(image, 3, ((2, 6), (4, 0)))

    value = screened(image[2:6])
    second[...] = value
    landed(edge)
    planes = outside([image[k] for k in (0, 1)], first) + [image[k] for k in range(2, 6)]
    planes = planes + outside([image[k] for k in (6, 7)], last)
    smooth = stencil(planes, stiff_ref, mass_ref)
    for k in range(PLANES):
        second[k] = second[k] + smooth[k]

    def fold(value):
        return value.reshape(CELLS // 8, 8, COLS)

    out_residual[...] = residual[2:6]
    out_image[...] = image[2:6]
    out_second[...] = second[...]
    r0 = fold(residual[2:6])
    scale = jnp.max(jnp.max(jnp.abs(r0), axis=0), axis=0, keepdims=True)
    scale = jnp.maximum(jnp.max(scale, axis=1, keepdims=True), 1e-30)
    inverse = 1.0 / scale
    r0 = r0 * inverse
    w = fold(image[2:6]) * inverse
    u = fold(second[...]) * inverse
    moments = [
        jnp.sum(jnp.sum(a * b, axis=0), axis=0, keepdims=True) for a, b in ((r0, r0), (r0, w), (w, w), (w, u))
    ]
    row = packed(moments, scale)

    for turn, arrived in enumerate(arrivals):
        count = len(peers[turn])
        sums[turn] = row
        arrived[count : count + 1, :] = row
        for slot, peer in enumerate(peers[turn]):
            pltpu.make_async_remote_copy(
                src_ref=sums.at[turn],
                dst_ref=arrived.at[pl.ds(slot, 1)],
                send_sem=sum_send.at[turn],
                recv_sem=sum_recv.at[turn],
                device_id=peer,
                device_id_type=MESH,
            ).start()
        whole = arrived.at[pl.ds(0, count)]
        pltpu.make_async_copy(whole, whole, sum_recv.at[turn]).wait()
        row = combine(arrived[...])

    lane = lax.broadcasted_iota(jnp.int32, (1, COLS), 1)
    m0, m1, m2, m3 = (
        jnp.sum(jnp.where(lane // 16 == k, row, 0.0), axis=1, keepdims=True) for k in range(4)
    )
    a0 = m0 / m1
    g = a0 * (m2 / m1)
    a1 = (g - 1.0) * m1 / (a0 * m3 - g * m2)
    c1 = a0 + a1 * g
    c2 = a1 * a0
    out_factor[...] = jnp.concatenate([jnp.broadcast_to(c, (1, COLS)) for c in (c1, c2)] * 4, axis=0)

    for copy in started:
        copy.wait_send()
    for turn, arrived in enumerate(arrivals):
        whole = arrived.at[pl.ds(0, len(peers[turn]))]
        pltpu.make_async_copy(whole, whole, sum_send.at[turn]).wait()


def body(right_side, initial_guess, point_cell, point_offset, point_weight, point_mask, block_count):
    slab = pltpu.VMEM((PLANES, ROWS, COLS), jnp.float32)
    vmem = pl.BlockSpec(memory_space=pltpu.VMEM)
    groups = []
    for axes in STAGES:
        size = 1
        for axis in axes:
            size *= SIZES[axis]
        groups.append(size)
    r0, w, u, factor = pl.pallas_call(
        kernel,
        out_shape=(slab, slab, slab, pltpu.VMEM((8, COLS), jnp.float32)),
        in_specs=[pl.BlockSpec(memory_space=pltpu.HBM)] * 6 + [pl.BlockSpec(memory_space=pltpu.SMEM)],
        out_specs=(vmem,) * 4,
        scratch_shapes=[
            pltpu.VMEM((PLANES, ROWS, COLS), jnp.float32),
            pltpu.VMEM((3, POINTS), jnp.int32),
            pltpu.VMEM((3, POINTS), jnp.float32),
            pltpu.VMEM((POINTS // COLS, COLS), jnp.float32),
            pltpu.VMEM((POINTS // COLS, COLS), jnp.int32),
            pltpu.VMEM((PLANES + 8, ROWS, COLS), jnp.float32),
            pltpu.VMEM((PLANES + 4, ROWS, COLS), jnp.float32),
            pltpu.VMEM((PLANES + 4, ROWS, COLS), jnp.float32),
            pltpu.VMEM((PLANES + 4, ROWS, COLS), jnp.float32),
            pltpu.VMEM((PLANES, ROWS, COLS), jnp.float32),
            pltpu.VMEM((PLANES, ROWS + 2 * EDGE, COLS), jnp.float32),
            pltpu.VMEM((PLANES, ROWS + 2 * EDGE, COLS), jnp.float32),
            pltpu.VMEM((2 * COLS, POINTS), jnp.bfloat16),
            pltpu.VMEM((ROWS, POINTS), jnp.float32),
            pltpu.VMEM((8, POINTS), jnp.float32),
            pltpu.VMEM((8, POINTS), jnp.float32),
            pltpu.VMEM((2 * CELLS, 2 * COLS), jnp.bfloat16),
            pltpu.VMEM((2 * CELLS, POINTS), jnp.bfloat16),
            pltpu.SemaphoreType.DMA((6,)),
            pltpu.SemaphoreType.DMA((4, 2)),
            pltpu.SemaphoreType.DMA((4, 2)),
            pltpu.SemaphoreType.DMA((len(STAGES),)),
            pltpu.SemaphoreType.DMA((len(STAGES),)),
            pltpu.VMEM((len(STAGES), 1, COLS), jnp.float32),
        ]
        + [pltpu.VMEM((size, COLS), jnp.float32) for size in groups],
        compiler_params=pltpu.CompilerParams(
            collective_id=0, has_side_effects=True, vmem_limit_bytes=56 * 1024 * 1024
        ),
        cost_estimate=pl.CostEstimate(flops=3_000_000_000, bytes_accessed=700_000, transcendentals=0),
    )(
        right_side, initial_guess, point_cell, point_offset,
        point_weight.reshape(POINTS // COLS, COLS), point_mask.reshape(POINTS // COLS, COLS), block_count,
    )
    c1, c2 = factor[0], factor[1]
    return initial_guess + c1 * r0 - c2 * w, r0 - c1 * w + c2 * u


def solution(mesh):
    placed = (
        P(("bricks", "pts"), None, None),
        P(("bricks", "pts"), None, None),
        P(None, ("bricks", "pts")),
        P(None, ("bricks", "pts")),
        P(("bricks", "pts")),
        P(("bricks", "pts")),
        P(("bricks", "pts")),
    )
    return jax.shard_map(
        body,
        mesh=mesh,
        in_specs=placed,
        out_specs=(P(("bricks", "pts"), None, None), P(("bricks", "pts"), None, None)),
        check_vma=False,
    )
```

```python
import functools

import jax
import jax.numpy as jnp
from jax import lax
from jax.experimental import pallas as pl
from jax.experimental.pallas import tpu as pltpu
from jax.sharding import PartitionSpec as P

MESH = pl.DeviceIdType.MESH

PLANES = 4
ROWS = 64
COLS = 128
CELLS = PLANES * ROWS
BLOCK = 256
BLOCKS = 8
POINTS = BLOCK * BLOCKS
EDGE = 8

SIZES = {"x": 4, "y": 4, "z": 8, "core": 2}
STAGES = (("x", "y", "core"), ("z",))


def spline_weights(offset):
    return (0.5 * (0.5 - offset) ** 2, 0.75 - offset * offset, 0.5 * (0.5 + offset) ** 2)


def coordinates():
    brick = lax.axis_index("bricks")
    return {
        "x": lax.axis_index("pts"),
        "y": brick // 16,
        "z": (brick // 2) % 8,
        "core": brick % 2,
    }


def device_of(place):
    return ((place["y"] * 8 + place["z"]) * 2 + place["core"], place["x"])


def stage_peers(here, axes):
    steps = [{}]
    for axis in axes:
        steps = [dict(step, **{axis: k}) for step in steps for k in range(SIZES[axis])]
    peers = []
    for step in steps[1:]:
        place = dict(here)
        for axis, k in step.items():
            if k:
                place[axis] = (here[axis] + k) % SIZES[axis]
        peers.append(device_of(place))
    return peers


def two_terms(value):
    high = value.astype(jnp.bfloat16)
    low = (value - high.astype(jnp.float32)).astype(jnp.bfloat16)
    return high, low


def block_row(ref, block):
    return jnp.concatenate([ref[2 * block : 2 * block + 1, :], ref[2 * block + 1 : 2 * block + 2, :]], axis=1)


def build_tables(cell_ref, offset_ref, weight_ref, mask_ref, count_ref, table_z, table_y, table_x, strength_ref):
    count = count_ref[0]
    for block in range(BLOCKS):
        lanes = pl.ds(block * BLOCK, BLOCK)

        def factors(axis):
            return cell_ref[axis : axis + 1, lanes], spline_weights(offset_ref[axis : axis + 1, lanes])

        def spread_out(cell, rows, parts):
            apart = lax.broadcasted_iota(jnp.int32, (rows, BLOCK), 0) - cell
            zero = jnp.zeros((rows, BLOCK), jnp.float32)
            before, at, after = apart == -1, apart == 0, apart == 1
            return [jnp.where(before, a, jnp.where(at, b, jnp.where(after, c, zero))) for a, b, c in parts]

        cell, parts = factors(2)
        terms = [two_terms(part) for part in parts]
        high, low = spread_out(
            cell,
            COLS,
            [[t[0].astype(jnp.float32) for t in terms], [t[1].astype(jnp.float32) for t in terms]],
        )
        table_z[0:COLS, lanes] = high.astype(jnp.bfloat16)
        table_z[COLS : 2 * COLS, lanes] = low.astype(jnp.bfloat16)
        cell, parts = factors(1)
        table_y[:, lanes] = spread_out(cell, ROWS, [parts])[0]
        cell, parts = factors(0)
        table_x[:, lanes] = spread_out(cell, 8, [parts])[0]
        alive = jnp.where(count > block, 1.0, 0.0)
        strength_ref[0:1, lanes] = (
            jnp.where(block_row(mask_ref, block) == 1, block_row(weight_ref, block), 0.0) * alive
        )


def screen(field, table_z, table_y, table_x, strength_ref, left_ref, spread_ref):
    high, low = two_terms(field)
    left_ref[0:CELLS, 0:COLS] = high
    left_ref[0:CELLS, COLS : 2 * COLS] = high
    left_ref[CELLS : 2 * CELLS, 0:COLS] = low
    left_ref[CELLS : 2 * CELLS, COLS : 2 * COLS] = low
    for block in range(BLOCKS):
        lanes = pl.ds(block * BLOCK, BLOCK)
        both = jnp.dot(left_ref[...], table_z[:, lanes], preferred_element_type=jnp.float32)
        sampled = (both[0:CELLS] + both[CELLS : 2 * CELLS]).reshape(PLANES, ROWS, BLOCK)
        along_y = table_y[:, lanes]
        along_x = table_x[:, lanes]
        total = jnp.zeros((8, BLOCK), jnp.float32)
        for plane in range(PLANES):
            summed = jnp.sum((sampled[plane] * along_y).reshape(ROWS // 8, 8, BLOCK), axis=0)
            total = total + summed * along_x[plane : plane + 1]
        values = jnp.sum(total, axis=0, keepdims=True) * strength_ref[0:1, lanes]
        for plane in range(PLANES):
            high, low = two_terms(along_y * (along_x[plane : plane + 1] * values))
            spread_ref[plane * ROWS : (plane + 1) * ROWS, lanes] = high
            spread_ref[CELLS + plane * ROWS : CELLS + (plane + 1) * ROWS, lanes] = low
    result = lax.dot_general(
        spread_ref[...], table_z[...], (((1,), (1,)), ((), ())), preferred_element_type=jnp.float32
    )
    result = result[0:CELLS] + result[CELLS : 2 * CELLS]
    return result[:, 0:COLS] + result[:, COLS : 2 * COLS]


MASS_TAPS = (1.0 / 120.0, 26.0 / 120.0, 66.0 / 120.0)
STIFF_TAPS = (-1.0 / 6.0, -1.0 / 3.0, 1.0)


def five(taps, values):
    return taps[2] * values[2] + taps[1] * (values[1] + values[3]) + taps[0] * (values[0] + values[4])


def own_part(taps, p):
    near, far = taps[1], taps[0]
    return [
        taps[2] * p[0] + near * p[1] + far * p[2],
        taps[2] * p[1] + near * (p[0] + p[2]) + far * p[3],
        taps[2] * p[2] + near * (p[1] + p[3]) + far * p[0],
        taps[2] * p[3] + near * p[2] + far * p[1],
    ]


def cross_part(taps, p):
    near, far = taps[1], taps[0]
    return [far * p[0] + near * p[1], far * p[1], far * p[2], near * p[2] + far * p[3]]


def outward_part(taps, p):
    near, far = taps[1], taps[0]
    return [far * p[0], near * p[0] + far * p[1], far * p[2] + near * p[3], far * p[3]]


def stencil(part, planes, stiff_ref, mass_ref):
    for k, (stiff_x, mass_x) in enumerate(zip(part(STIFF_TAPS, planes), part(MASS_TAPS, planes))):
        stiff_ref[k, EDGE : EDGE + ROWS, :] = stiff_x
        mass_ref[k, EDGE : EDGE + ROWS, :] = mass_x
    lane = lax.broadcasted_iota(jnp.int32, (ROWS, COLS), 1)

    def along_z(value):
        return [
            jnp.where(lane >= 2, pltpu.roll(value, 2, 1), 0.0),
            jnp.where(lane >= 1, pltpu.roll(value, 1, 1), 0.0),
            value,
            jnp.where(lane < COLS - 1, pltpu.roll(value, COLS - 1, 1), 0.0),
            jnp.where(lane < COLS - 2, pltpu.roll(value, COLS - 2, 1), 0.0),
        ]

    out = []
    for k in range(PLANES):
        stiff_x = [stiff_ref[k, EDGE - 2 + s : EDGE - 2 + s + ROWS, :] for s in range(5)]
        mass_x = [mass_ref[k, EDGE - 2 + s : EDGE - 2 + s + ROWS, :] for s in range(5)]
        mixed = five(MASS_TAPS, stiff_x) + five(STIFF_TAPS, mass_x)
        out.append(five(MASS_TAPS, along_z(mixed)) + five(STIFF_TAPS, along_z(five(MASS_TAPS, mass_x))))
    return out


def packed(moments, scale):
    lane = lax.broadcasted_iota(jnp.int32, (1, COLS), 1)
    row = jnp.broadcast_to(scale, (1, COLS))
    for k, moment in enumerate(moments):
        for shift in (64, 32, 16):
            moment = moment + pltpu.roll(moment, shift, 1)
        row = jnp.where(lane // 16 == k, moment, row)
    return row


def combine(rows):
    lane = lax.broadcasted_iota(jnp.int32, rows.shape, 1)
    scales = jnp.max(jnp.where(lane >= 64, rows, 0.0), axis=1, keepdims=True)
    largest = jnp.max(scales, axis=0, keepdims=True)
    ratio = scales / largest
    total = jnp.sum(rows * (ratio * ratio), axis=0, keepdims=True)
    return jnp.where(lane[0:1] >= 64, largest, total)


def kernel(
    right_in, guess_in, cell_in, offset_in, weight_in, mask_in, count_ref,
    residual, image, second, out_factor,
    right_ref, cell_ref, offset_ref, weight_ref, mask_ref,
    guess, known, partial, outward, stiff_ref, mass_ref,
    table_z, table_y, table_x, strength_ref, left_ref, spread_ref,
    load_sem, halo_send, halo_recv, sum_send, sum_recv, sums, *arrivals,
):
    here = coordinates()
    device = lax.axis_index("bricks") * 4 + lax.axis_index("pts")
    before, after = (device + 255) % 256, (device + 1) % 256
    left, right = (before // 4, before % 4), (after // 4, after % 4)
    peers = [stage_peers(here, axes) for axes in STAGES]

    barrier = pltpu.get_barrier_semaphore()
    greeted = [left, right] + [p for stage in peers for p in stage]
    for peer in greeted[0:2]:
        pl.semaphore_signal(barrier, inc=1, device_id=peer, device_id_type=MESH)
    loads = [
        pltpu.make_async_copy(source, target, load_sem.at[k])
        for k, (source, target) in enumerate((
            (cell_in, cell_ref),
            (offset_in, offset_ref),
            (weight_in, weight_ref),
            (mask_in, mask_ref),
            (guess_in, guess.at[pl.ds(2, PLANES)]),
            (right_in, right_ref),
        ))
    ]
    for load in loads:
        load.start()
    for peer in greeted[2:]:
        pl.semaphore_signal(barrier, inc=1, device_id=peer, device_id_type=MESH)

    first, last = device == 0, device == 255
    for ref in (stiff_ref, mass_ref):
        ref[:, 0:EDGE, :] = jnp.zeros((PLANES, EDGE, COLS), jnp.float32)
        ref[:, EDGE + ROWS : 2 * EDGE + ROWS, :] = jnp.zeros((PLANES, EDGE, COLS), jnp.float32)
    for load in loads[0:4]:
        load.wait()
    build_tables(cell_ref, offset_ref, weight_ref, mask_ref, count_ref, table_z, table_y, table_x, strength_ref)
    tables = (table_z, table_y, table_x, strength_ref, left_ref, spread_ref)

    loads[4].wait()
    pl.semaphore_wait(barrier, len(greeted))
    started = []

    def send(field, turn):
        copies = []
        for side, (source, target) in enumerate(((2, 6), (4, 0))):
            copy = pltpu.make_async_remote_copy(
                src_ref=field.at[pl.ds(source, 2)],
                dst_ref=field.at[pl.ds(target, 2)],
                send_sem=halo_send.at[turn, side],
                recv_sem=halo_recv.at[turn, side],
                device_id=(left, right)[side],
                device_id_type=MESH,
            )
            copy.start()
            copies.append(copy)
        started.extend(copies)
        return copies

    def landed(copies):
        for copy in copies:
            copy.wait_recv()

    def screened(field):
        return screen(field.reshape(CELLS, COLS), *tables).reshape(PLANES, ROWS, COLS)

    def smooth(part, planes):
        return stencil(part, planes, stiff_ref, mass_ref)

    def four(ref, at):
        return [ref[at + k] for k in range(PLANES)]

    def beside(field, added):
        planes = [field[k] for k in (0, 1, 6, 7)]
        if added is not None:
            planes = [p + outward[k] for k, p in enumerate(planes)]
        return [jnp.where(first, 0.0, p) for p in planes[0:2]] + [jnp.where(last, 0.0, p) for p in planes[2:4]]

    def fold(value):
        return value.reshape(CELLS // 8, 8, COLS)

    def dot(a, b):
        return jnp.sum(fold(a) * fold(b), axis=0)

    copies = send(guess, 0)
    own = smooth(own_part, four(guess, 2))
    loads[5].wait()
    for k in range(PLANES):
        known[2 + k] = right_ref[k] - own[k]
    known[2:6] = known[2:6] - screened(guess[2:6])
    edge = send(known, 1)
    added = smooth(outward_part, four(guess, 2))
    for k in range(PLANES):
        outward[k] = -added[k]

    landed(copies)
    added = smooth(cross_part, beside(guess, None))
    for k in range(PLANES):
        residual[k] = known[2 + k] - added[k]
    own = smooth(own_part, four(residual, 0))
    for k in range(PLANES):
        partial[2 + k] = own[k]
    partial[2:6] = partial[2:6] + screened(residual[...])
    copies = send(partial, 2)

    landed(edge)
    added = smooth(cross_part, beside(known, outward))
    for k in range(PLANES):
        image[k] = partial[2 + k] + added[k]
    added = smooth(outward_part, four(residual, 0))
    for k in range(PLANES):
        outward[k] = added[k]
    own = smooth(own_part, four(image, 0))
    for k in range(PLANES):
        second[k] = own[k]
    second[...] = second[...] + screened(image[...])

    scale = jnp.max(jnp.max(jnp.abs(fold(residual[...])), axis=0), axis=0, keepdims=True)
    scale = jnp.maximum(jnp.max(scale, axis=1, keepdims=True), 1e-30)
    inverse = 1.0 / scale
    r0 = residual[...] * inverse
    w = image[...] * inverse
    u = second[...] * inverse
    moments = [dot(r0, r0), dot(r0, w), dot(w, w)]
    last_moment = dot(w, u)

    landed(copies)
    added = smooth(cross_part, beside(partial, outward))
    for k in range(PLANES):
        second[k] = second[k] + added[k]
        last_moment = last_moment + jnp.sum(
            ((image[k] * inverse) * (added[k] * inverse)).reshape(ROWS // 8, 8, COLS), axis=0
        )
    moments = [jnp.sum(m, axis=0, keepdims=True) for m in moments + [last_moment]]
    row = packed(moments, scale)

    for turn, arrived in enumerate(arrivals):
        count = len(peers[turn])
        sums[turn] = row
        arrived[count : count + 1, :] = row
        for slot, peer in enumerate(peers[turn]):
            pltpu.make_async_remote_copy(
                src_ref=sums.at[turn],
                dst_ref=arrived.at[pl.ds(slot, 1)],
                send_sem=sum_send.at[turn],
                recv_sem=sum_recv.at[turn],
                device_id=peer,
                device_id_type=MESH,
            ).start()
        whole = arrived.at[pl.ds(0, count)]
        pltpu.make_async_copy(whole, whole, sum_recv.at[turn]).wait()
        row = combine(arrived[...])

    lane = lax.broadcasted_iota(jnp.int32, (1, COLS), 1)
    m0, m1, m2, m3 = (
        jnp.sum(jnp.where(lane // 16 == k, row, 0.0), axis=1, keepdims=True) for k in range(4)
    )
    a0 = m0 / m1
    g = a0 * (m2 / m1)
    a1 = (g - 1.0) * m1 / (a0 * m3 - g * m2)
    c1 = a0 + a1 * g
    c2 = a1 * a0
    out_factor[...] = jnp.concatenate([jnp.broadcast_to(c, (1, COLS)) for c in (c1, c2)] * 4, axis=0)

    for copy in started:
        copy.wait_send()
    for turn, arrived in enumerate(arrivals):
        whole = arrived.at[pl.ds(0, len(peers[turn]))]
        pltpu.make_async_copy(whole, whole, sum_send.at[turn]).wait()


def body(right_side, initial_guess, point_cell, point_offset, point_weight, point_mask, block_count):
    slab = pltpu.VMEM((PLANES, ROWS, COLS), jnp.float32)
    vmem = pl.BlockSpec(memory_space=pltpu.VMEM)
    groups = []
    for axes in STAGES:
        size = 1
        for axis in axes:
            size *= SIZES[axis]
        groups.append(size)
    r0, w, u, factor = pl.pallas_call(
        kernel,
        out_shape=(slab, slab, slab, pltpu.VMEM((8, COLS), jnp.float32)),
        in_specs=[pl.BlockSpec(memory_space=pltpu.HBM)] * 6 + [pl.BlockSpec(memory_space=pltpu.SMEM)],
        out_specs=(vmem,) * 4,
        scratch_shapes=[
            pltpu.VMEM((PLANES, ROWS, COLS), jnp.float32),
            pltpu.VMEM((3, POINTS), jnp.int32),
            pltpu.VMEM((3, POINTS), jnp.float32),
            pltpu.VMEM((POINTS // COLS, COLS), jnp.float32),
            pltpu.VMEM((POINTS // COLS, COLS), jnp.int32),
            pltpu.VMEM((PLANES + 4, ROWS, COLS), jnp.float32),
            pltpu.VMEM((PLANES + 4, ROWS, COLS), jnp.float32),
            pltpu.VMEM((PLANES + 4, ROWS, COLS), jnp.float32),
            pltpu.VMEM((PLANES, ROWS, COLS), jnp.float32),
            pltpu.VMEM((PLANES, ROWS + 2 * EDGE, COLS), jnp.float32),
            pltpu.VMEM((PLANES, ROWS + 2 * EDGE, COLS), jnp.float32),
            pltpu.VMEM((2 * COLS, POINTS), jnp.bfloat16),
            pltpu.VMEM((ROWS, POINTS), jnp.float32),
            pltpu.VMEM((8, POINTS), jnp.float32),
            pltpu.VMEM((8, POINTS), jnp.float32),
            pltpu.VMEM((2 * CELLS, 2 * COLS), jnp.bfloat16),
            pltpu.VMEM((2 * CELLS, POINTS), jnp.bfloat16),
            pltpu.SemaphoreType.DMA((6,)),
            pltpu.SemaphoreType.DMA((3, 2)),
            pltpu.SemaphoreType.DMA((3, 2)),
            pltpu.SemaphoreType.DMA((len(STAGES),)),
            pltpu.SemaphoreType.DMA((len(STAGES),)),
            pltpu.VMEM((len(STAGES), 1, COLS), jnp.float32),
        ]
        + [pltpu.VMEM((size, COLS), jnp.float32) for size in groups],
        compiler_params=pltpu.CompilerParams(
            collective_id=0, has_side_effects=True, vmem_limit_bytes=56 * 1024 * 1024
        ),
        cost_estimate=pl.CostEstimate(flops=3_000_000_000, bytes_accessed=700_000, transcendentals=0),
    )(
        right_side, initial_guess, point_cell, point_offset,
        point_weight.reshape(POINTS // COLS, COLS), point_mask.reshape(POINTS // COLS, COLS), block_count,
    )
    c1, c2 = factor[0], factor[1]
    return initial_guess + c1 * r0 - c2 * w, r0 - c1 * w + c2 * u


def solution(mesh):
    placed = (
        P(("bricks", "pts"), None, None),
        P(("bricks", "pts"), None, None),
        P(None, ("bricks", "pts")),
        P(None, ("bricks", "pts")),
        P(("bricks", "pts")),
        P(("bricks", "pts")),
        P(("bricks", "pts")),
    )
    return jax.shard_map(
        body,
        mesh=mesh,
        in_specs=placed,
        out_specs=(P(("bricks", "pts"), None, None), P(("bricks", "pts"), None, None)),
        check_vma=False,
    )
```

```python
import functools

import jax
import jax.numpy as jnp
from jax import lax
from jax.experimental import pallas as pl
from jax.experimental.pallas import tpu as pltpu
from jax.sharding import PartitionSpec as P

MESH = pl.DeviceIdType.MESH

PLANES = 4
ROWS = 64
COLS = 128
CELLS = PLANES * ROWS
BLOCK = 256
BLOCKS = 8
POINTS = BLOCK * BLOCKS
EDGE = 8

SIZES = {"x": 4, "y": 4, "z": 8, "core": 2}
STAGES = (("core",), ("x", "y", "z"))
GREETED = ("y", "z")
TOLD = ("x", "core")


def spline_weights(offset):
    return (0.5 * (0.5 - offset) ** 2, 0.75 - offset * offset, 0.5 * (0.5 + offset) ** 2)


def coordinates():
    brick = lax.axis_index("bricks")
    return {
        "x": lax.axis_index("pts"),
        "y": brick // 16,
        "z": (brick // 2) % 8,
        "core": brick % 2,
    }


def device_of(place):
    return ((place["y"] * 8 + place["z"]) * 2 + place["core"], place["x"])


def stage_peers(here, axes):
    steps = [{}]
    for axis in axes:
        steps = [dict(step, **{axis: k}) for step in steps for k in range(SIZES[axis])]
    peers = []
    far = lambda step: sum(min(k, SIZES[axis] - k) for axis, k in step.items())
    for step in sorted(steps[1:], key=far, reverse=True):
        place = dict(here)
        for axis, k in step.items():
            if k:
                place[axis] = (here[axis] + k) % SIZES[axis]
        peers.append(device_of(place))
    return peers


def two_terms(value):
    high = value.astype(jnp.bfloat16)
    low = (value - high.astype(jnp.float32)).astype(jnp.bfloat16)
    return high, low


def block_row(ref, block):
    return jnp.concatenate([ref[2 * block : 2 * block + 1, :], ref[2 * block + 1 : 2 * block + 2, :]], axis=1)


def build_tables(cell_ref, offset_ref, weight_ref, mask_ref, count_ref, table_z, table_y, table_x, strength_ref):
    count = count_ref[0:1, 0:1]
    for block in range(BLOCKS):
        lanes = pl.ds(block * BLOCK, BLOCK)

        def factors(axis):
            return cell_ref[axis : axis + 1, lanes], spline_weights(offset_ref[axis : axis + 1, lanes])

        def spread_out(cell, rows, parts):
            apart = lax.broadcasted_iota(jnp.int32, (rows, BLOCK), 0) - cell
            zero = jnp.zeros((rows, BLOCK), jnp.float32)
            before, at, after = apart == -1, apart == 0, apart == 1
            return [jnp.where(before, a, jnp.where(at, b, jnp.where(after, c, zero))) for a, b, c in parts]

        cell, parts = factors(2)
        terms = [two_terms(part) for part in parts]
        high, low = spread_out(
            cell,
            COLS,
            [[t[0].astype(jnp.float32) for t in terms], [t[1].astype(jnp.float32) for t in terms]],
        )
        table_z[0:COLS, lanes] = high.astype(jnp.bfloat16)
        table_z[COLS : 2 * COLS, lanes] = low.astype(jnp.bfloat16)
        cell, parts = factors(1)
        table_y[:, lanes] = spread_out(cell, ROWS, [parts])[0]
        cell, parts = factors(0)
        table_x[:, lanes] = spread_out(cell, 8, [parts])[0]
        alive = jnp.where(count > block, 1.0, 0.0)
        strength_ref[0:1, lanes] = (
            jnp.where(block_row(mask_ref, block) == 1, block_row(weight_ref, block), 0.0) * alive
        )


def screen(field, table_z, table_y, table_x, strength_ref, left_ref, spread_ref):
    high, low = two_terms(field)
    left_ref[0:CELLS, 0:COLS] = high
    left_ref[0:CELLS, COLS : 2 * COLS] = high
    left_ref[CELLS : 2 * CELLS, 0:COLS] = low
    left_ref[CELLS : 2 * CELLS, COLS : 2 * COLS] = low
    for block in range(BLOCKS):
        lanes = pl.ds(block * BLOCK, BLOCK)
        both = jnp.dot(left_ref[...], table_z[:, lanes], preferred_element_type=jnp.float32)
        sampled = (both[0:CELLS] + both[CELLS : 2 * CELLS]).reshape(PLANES, ROWS, BLOCK)
        along_y = table_y[:, lanes]
        along_x = table_x[:, lanes]
        total = jnp.zeros((8, BLOCK), jnp.float32)
        for plane in range(PLANES):
            summed = jnp.sum((sampled[plane] * along_y).reshape(ROWS // 8, 8, BLOCK), axis=0)
            total = total + summed * along_x[plane : plane + 1]
        values = jnp.sum(total, axis=0, keepdims=True) * strength_ref[0:1, lanes]
        for plane in range(PLANES):
            high, low = two_terms(along_y * (along_x[plane : plane + 1] * values))
            spread_ref[plane * ROWS : (plane + 1) * ROWS, lanes] = high
            spread_ref[CELLS + plane * ROWS : CELLS + (plane + 1) * ROWS, lanes] = low
    result = lax.dot_general(
        spread_ref[...], table_z[...], (((1,), (1,)), ((), ())), preferred_element_type=jnp.float32
    )
    result = result[0:CELLS] + result[CELLS : 2 * CELLS]
    return result[:, 0:COLS] + result[:, COLS : 2 * COLS]


MASS_TAPS = (1.0 / 120.0, 26.0 / 120.0, 66.0 / 120.0)
STIFF_TAPS = (-1.0 / 6.0, -1.0 / 3.0, 1.0)


def five(taps, values):
    return taps[2] * values[2] + taps[1] * (values[1] + values[3]) + taps[0] * (values[0] + values[4])


def own_part(taps, p):
    near, far = taps[1], taps[0]
    return [
        taps[2] * p[0] + near * p[1] + far * p[2],
        taps[2] * p[1] + near * (p[0] + p[2]) + far * p[3],
        taps[2] * p[2] + near * (p[1] + p[3]) + far * p[0],
        taps[2] * p[3] + near * p[2] + far * p[1],
    ]


def cross_part(taps, p):
    near, far = taps[1], taps[0]
    return [far * p[0] + near * p[1], far * p[1], far * p[2], near * p[2] + far * p[3]]


def outward_part(taps, p):
    near, far = taps[1], taps[0]
    return [far * p[0], near * p[0] + far * p[1], far * p[2] + near * p[3], far * p[3]]


def stencil(part, planes, stiff_ref, mass_ref):
    for k, (stiff_x, mass_x) in enumerate(zip(part(STIFF_TAPS, planes), part(MASS_TAPS, planes))):
        stiff_ref[k, EDGE : EDGE + ROWS, :] = stiff_x
        mass_ref[k, EDGE : EDGE + ROWS, :] = mass_x
    lane = lax.broadcasted_iota(jnp.int32, (ROWS, COLS), 1)

    def along_z(value):
        return [
            jnp.where(lane >= 2, pltpu.roll(value, 2, 1), 0.0),
            jnp.where(lane >= 1, pltpu.roll(value, 1, 1), 0.0),
            value,
            jnp.where(lane < COLS - 1, pltpu.roll(value, COLS - 1, 1), 0.0),
            jnp.where(lane < COLS - 2, pltpu.roll(value, COLS - 2, 1), 0.0),
        ]

    out = []
    for k in range(PLANES):
        stiff_x = [stiff_ref[k, EDGE - 2 + s : EDGE - 2 + s + ROWS, :] for s in range(5)]
        mass_x = [mass_ref[k, EDGE - 2 + s : EDGE - 2 + s + ROWS, :] for s in range(5)]
        mixed = five(MASS_TAPS, stiff_x) + five(STIFF_TAPS, mass_x)
        out.append(five(MASS_TAPS, along_z(mixed)) + five(STIFF_TAPS, along_z(five(MASS_TAPS, mass_x))))
    return out


def folded(moment, lanes):
    shift = COLS // 2
    while shift >= lanes:
        moment = moment + pltpu.roll(moment, shift, 1)
        shift //= 2
    return moment


def lane_groups():
    lane = lax.broadcasted_iota(jnp.int32, (1, COLS), 1)
    return [lane // 8 == 4, lane // 8 == 5, lane // 8 == 6, lane < 32]


def combine(rows):
    lane = lax.broadcasted_iota(jnp.int32, (1, COLS), 1)
    largest = jnp.max(rows, axis=0, keepdims=True)
    ratio = pltpu.roll(rows * (1.0 / largest), COLS // 2, 1)
    total = jnp.sum(rows * (ratio * ratio), axis=0, keepdims=True)
    return jnp.where(lane >= 64, largest, total)


def kernel(
    right_in, guess_in, cell_in, offset_in, weight_in, mask_in, count_ref,
    residual, image, second, out_factor,
    right_ref, cell_ref, offset_ref, weight_ref, mask_ref,
    guess, known, partial, outward, stiff_ref, mass_ref,
    table_z, table_y, table_x, strength_ref, left_ref, spread_ref,
    load_sem, halo_send, halo_recv, sum_send, sum_recv, entered, sums, *arrivals,
):
    here = coordinates()
    device = lax.axis_index("bricks") * 4 + lax.axis_index("pts")
    before, after = (device + 255) % 256, (device + 1) % 256
    left, right = (before // 4, before % 4), (after // 4, after % 4)
    peers = [stage_peers(here, axes) for axes in STAGES]

    barrier = pltpu.get_barrier_semaphore()
    told = stage_peers(here, TOLD)
    greeted = [left, right] + stage_peers(here, GREETED) + told
    for peer in greeted[0:2]:
        pl.semaphore_signal(barrier, inc=1, device_id=peer, device_id_type=MESH)
    loads = [
        pltpu.make_async_copy(source, target, load_sem.at[k])
        for k, (source, target) in enumerate((
            (cell_in, cell_ref),
            (offset_in, offset_ref),
            (weight_in, weight_ref),
            (mask_in, mask_ref),
            (guess_in, guess.at[pl.ds(2, PLANES)]),
            (right_in, right_ref),
        ))
    ]
    for load in loads:
        load.start()
    for peer in greeted[2:]:
        pl.semaphore_signal(barrier, inc=1, device_id=peer, device_id_type=MESH)

    first, last = device == 0, device == 255
    for ref in (stiff_ref, mass_ref):
        ref[:, 0:EDGE, :] = jnp.zeros((PLANES, EDGE, COLS), jnp.float32)
        ref[:, EDGE + ROWS : 2 * EDGE + ROWS, :] = jnp.zeros((PLANES, EDGE, COLS), jnp.float32)
    for load in loads[0:4]:
        load.wait()
    build_tables(cell_ref, offset_ref, weight_ref, mask_ref, count_ref, table_z, table_y, table_x, strength_ref)
    tables = (table_z, table_y, table_x, strength_ref, left_ref, spread_ref)

    loads[4].wait()
    pl.semaphore_wait(barrier, len(greeted))
    started = []

    def send(field, turn):
        copies = []
        for side, (source, target) in enumerate(((2, 6), (4, 0))):
            copy = pltpu.make_async_remote_copy(
                src_ref=field.at[pl.ds(source, 2)],
                dst_ref=field.at[pl.ds(target, 2)],
                send_sem=halo_send.at[turn, side],
                recv_sem=halo_recv.at[turn, side],
                device_id=(left, right)[side],
                device_id_type=MESH,
            )
            copy.start()
            copies.append(copy)
        started.extend(copies)
        return copies

    def landed(copies):
        for copy in copies:
            copy.wait_recv()

    def screened(field):
        return screen(field.reshape(CELLS, COLS), *tables).reshape(PLANES, ROWS, COLS)

    def smooth(part, planes):
        return stencil(part, planes, stiff_ref, mass_ref)

    def four(ref, at):
        return [ref[at + k] for k in range(PLANES)]

    def beside(field, added):
        planes = [field[k] for k in (0, 1, 6, 7)]
        if added is not None:
            planes = [p + outward[k] for k, p in enumerate(planes)]
        return [jnp.where(first, 0.0, p) for p in planes[0:2]] + [jnp.where(last, 0.0, p) for p in planes[2:4]]

    def fold(value):
        return value.reshape(CELLS // 8, 8, COLS)

    def dot(a, b):
        return jnp.sum(fold(a) * fold(b), axis=0)

    copies = send(guess, 0)
    for peer in told:
        pl.semaphore_signal(entered, inc=1, device_id=peer, device_id_type=MESH)
    own = smooth(own_part, four(guess, 2))
    loads[5].wait()
    for k in range(PLANES):
        known[2 + k] = right_ref[k] - own[k]
    known[2:6] = known[2:6] - screened(guess[2:6])
    edge = send(known, 1)
    added = smooth(outward_part, four(guess, 2))
    for k in range(PLANES):
        outward[k] = -added[k]

    landed(copies)
    added = smooth(cross_part, beside(guess, None))
    for k in range(PLANES):
        residual[k] = known[2 + k] - added[k]
    own = smooth(own_part, four(residual, 0))
    for k in range(PLANES):
        partial[2 + k] = own[k]
    partial[2:6] = partial[2:6] + screened(residual[...])
    copies = send(partial, 2)

    landed(edge)
    added = smooth(cross_part, beside(known, outward))
    for k in range(PLANES):
        image[k] = partial[2 + k] + added[k]
    added = smooth(outward_part, four(residual, 0))
    for k in range(PLANES):
        outward[k] = added[k]
    own = smooth(own_part, four(image, 0))
    for k in range(PLANES):
        second[k] = own[k]
    second[...] = second[...] + screened(image[...])

    scale = jnp.max(jnp.max(jnp.abs(fold(residual[...])), axis=0), axis=0, keepdims=True)
    scale = jnp.maximum(jnp.max(scale, axis=1, keepdims=True), 1e-30)
    inverse = 1.0 / scale
    r0 = residual[...] * inverse
    w = image[...] * inverse
    u = second[...] * inverse
    groups = lane_groups()
    row = jnp.where(lax.broadcasted_iota(jnp.int32, (1, COLS), 1) >= 64, scale, 0.0)
    for group, a, b in zip(groups, (r0, r0, w), (r0, w, w)):
        row = jnp.where(group, folded(jnp.sum(dot(a, b), axis=0, keepdims=True), 8), row)
    last_moment = dot(w, u)

    landed(copies)
    added = smooth(cross_part, beside(partial, outward))
    for k in range(PLANES):
        second[k] = second[k] + added[k]
        last_moment = last_moment + jnp.sum(
            ((image[k] * inverse) * (added[k] * inverse)).reshape(ROWS // 8, 8, COLS), axis=0
        )
    row = jnp.where(groups[3], folded(jnp.sum(last_moment, axis=0, keepdims=True), 32), row)
    pl.semaphore_wait(entered, len(told))

    for turn, arrived in enumerate(arrivals):
        count = len(peers[turn])
        sums[turn] = row
        arrived[count : count + 1, :] = row
        for slot, peer in enumerate(peers[turn]):
            pltpu.make_async_remote_copy(
                src_ref=sums.at[turn],
                dst_ref=arrived.at[pl.ds(slot, 1)],
                send_sem=sum_send.at[turn],
                recv_sem=sum_recv.at[turn],
                device_id=peer,
                device_id_type=MESH,
            ).start()
        whole = arrived.at[pl.ds(0, count)]
        pltpu.make_async_copy(whole, whole, sum_recv.at[turn]).wait()
        row = combine(arrived[...])

    m0, m1, m2, m3 = (jnp.sum(jnp.where(group, row, 0.0), axis=1, keepdims=True) for group in groups)
    a0 = m0 / m1
    g = a0 * (m2 / m1)
    a1 = (g - 1.0) * m1 / (a0 * m3 - g * m2)
    c1 = a0 + a1 * g
    c2 = a1 * a0
    out_factor[...] = jnp.concatenate([jnp.broadcast_to(c, (1, COLS)) for c in (c1, c2)] * 4, axis=0)

    for copy in started:
        copy.wait_send()
    for turn, arrived in enumerate(arrivals):
        whole = arrived.at[pl.ds(0, len(peers[turn]))]
        pltpu.make_async_copy(whole, whole, sum_send.at[turn]).wait()


def body(right_side, initial_guess, point_cell, point_offset, point_weight, point_mask, block_count):
    slab = pltpu.VMEM((PLANES, ROWS, COLS), jnp.float32)
    vmem = pl.BlockSpec(memory_space=pltpu.VMEM)
    groups = []
    for axes in STAGES:
        size = 1
        for axis in axes:
            size *= SIZES[axis]
        groups.append(size)
    r0, w, u, factor = pl.pallas_call(
        kernel,
        out_shape=(slab, slab, slab, pltpu.VMEM((8, COLS), jnp.float32)),
        in_specs=[pl.BlockSpec(memory_space=pltpu.HBM)] * 6 + [vmem],
        out_specs=(vmem,) * 4,
        scratch_shapes=[
            pltpu.VMEM((PLANES, ROWS, COLS), jnp.float32),
            pltpu.VMEM((3, POINTS), jnp.int32),
            pltpu.VMEM((3, POINTS), jnp.float32),
            pltpu.VMEM((POINTS // COLS, COLS), jnp.float32),
            pltpu.VMEM((POINTS // COLS, COLS), jnp.int32),
            pltpu.VMEM((PLANES + 4, ROWS, COLS), jnp.float32),
            pltpu.VMEM((PLANES + 4, ROWS, COLS), jnp.float32),
            pltpu.VMEM((PLANES + 4, ROWS, COLS), jnp.float32),
            pltpu.VMEM((PLANES, ROWS, COLS), jnp.float32),
            pltpu.VMEM((PLANES, ROWS + 2 * EDGE, COLS), jnp.float32),
            pltpu.VMEM((PLANES, ROWS + 2 * EDGE, COLS), jnp.float32),
            pltpu.VMEM((2 * COLS, POINTS), jnp.bfloat16),
            pltpu.VMEM((ROWS, POINTS), jnp.float32),
            pltpu.VMEM((8, POINTS), jnp.float32),
            pltpu.VMEM((8, POINTS), jnp.float32),
            pltpu.VMEM((2 * CELLS, 2 * COLS), jnp.bfloat16),
            pltpu.VMEM((2 * CELLS, POINTS), jnp.bfloat16),
            pltpu.SemaphoreType.DMA((6,)),
            pltpu.SemaphoreType.DMA((3, 2)),
            pltpu.SemaphoreType.DMA((3, 2)),
            pltpu.SemaphoreType.DMA((len(STAGES),)),
            pltpu.SemaphoreType.DMA((len(STAGES),)),
            pltpu.SemaphoreType.REGULAR,
            pltpu.VMEM((len(STAGES), 1, COLS), jnp.float32),
        ]
        + [pltpu.VMEM((size, COLS), jnp.float32) for size in groups],
        compiler_params=pltpu.CompilerParams(
            collective_id=0, has_side_effects=True, vmem_limit_bytes=56 * 1024 * 1024
        ),
        cost_estimate=pl.CostEstimate(flops=3_000_000_000, bytes_accessed=700_000, transcendentals=0),
    )(
        right_side, initial_guess, point_cell, point_offset,
        point_weight.reshape(POINTS // COLS, COLS), point_mask.reshape(POINTS // COLS, COLS), block_count.reshape(1, 1),
    )
    c1, c2 = factor[0], factor[1]
    return initial_guess + c1 * r0 - c2 * w, r0 - c1 * w + c2 * u


def solution(mesh):
    placed = (
        P(("bricks", "pts"), None, None),
        P(("bricks", "pts"), None, None),
        P(None, ("bricks", "pts")),
        P(None, ("bricks", "pts")),
        P(("bricks", "pts")),
        P(("bricks", "pts")),
        P(("bricks", "pts")),
    )
    return jax.shard_map(
        body,
        mesh=mesh,
        in_specs=placed,
        out_specs=(P(("bricks", "pts"), None, None), P(("bricks", "pts"), None, None)),
        check_vma=False,
    )
```

```python
import functools

import jax
import jax.numpy as jnp
from jax import lax
from jax.experimental import pallas as pl
from jax.experimental.pallas import tpu as pltpu
from jax.sharding import PartitionSpec as P

MESH = pl.DeviceIdType.MESH

PLANES = 4
ROWS = 64
COLS = 128
CELLS = PLANES * ROWS
BLOCK = 256
BLOCKS = 8
POINTS = BLOCK * BLOCKS
EDGE = 8

SIZES = {"x": 4, "y": 4, "z": 8, "core": 2}
STAGES = (("core",), ("x", "y", "z"))


def spline_weights(offset):
    return (0.5 * (0.5 - offset) ** 2, 0.75 - offset * offset, 0.5 * (0.5 + offset) ** 2)


def coordinates():
    brick = lax.axis_index("bricks")
    return {
        "x": lax.axis_index("pts"),
        "y": brick // 16,
        "z": (brick // 2) % 8,
        "core": brick % 2,
    }


def device_of(place):
    return ((place["y"] * 8 + place["z"]) * 2 + place["core"], place["x"])


def stage_peers(here, axes):
    steps = [{}]
    for axis in axes:
        steps = [dict(step, **{axis: k}) for step in steps for k in range(SIZES[axis])]
    peers = []
    far = lambda step: sum(min(k, SIZES[axis] - k) for axis, k in step.items())
    for step in sorted(steps[1:], key=far, reverse=True):
        place = dict(here)
        for axis, k in step.items():
            if k:
                place[axis] = (here[axis] + k) % SIZES[axis]
        peers.append(device_of(place))
    return peers


def two_terms(value):
    high = value.astype(jnp.bfloat16)
    low = (value - high.astype(jnp.float32)).astype(jnp.bfloat16)
    return high, low


def block_row(ref, block):
    return jnp.concatenate([ref[2 * block : 2 * block + 1, :], ref[2 * block + 1 : 2 * block + 2, :]], axis=1)


def build_tables(cell_ref, offset_ref, weight_ref, mask_ref, count_ref, table_z, table_y, table_x, strength_ref):
    count = count_ref[0:1, 0:1]
    for block in range(BLOCKS):
        lanes = pl.ds(block * BLOCK, BLOCK)

        def factors(axis):
            return cell_ref[axis : axis + 1, lanes], spline_weights(offset_ref[axis : axis + 1, lanes])

        def spread_out(cell, rows, parts):
            apart = lax.broadcasted_iota(jnp.int32, (rows, BLOCK), 0) - cell
            zero = jnp.zeros((rows, BLOCK), jnp.float32)
            before, at, after = apart == -1, apart == 0, apart == 1
            return [jnp.where(before, a, jnp.where(at, b, jnp.where(after, c, zero))) for a, b, c in parts]

        cell, parts = factors(2)
        terms = [two_terms(part) for part in parts]
        high, low = spread_out(
            cell,
            COLS,
            [[t[0].astype(jnp.float32) for t in terms], [t[1].astype(jnp.float32) for t in terms]],
        )
        table_z[0:COLS, lanes] = high.astype(jnp.bfloat16)
        table_z[COLS : 2 * COLS, lanes] = low.astype(jnp.bfloat16)
        cell, parts = factors(1)
        table_y[:, lanes] = spread_out(cell, ROWS, [parts])[0]
        cell, parts = factors(0)
        table_x[:, lanes] = spread_out(cell, 8, [parts])[0]
        alive = jnp.where(count > block, 1.0, 0.0)
        strength_ref[0:1, lanes] = (
            jnp.where(block_row(mask_ref, block) == 1, block_row(weight_ref, block), 0.0) * alive
        )


def screen(field, table_z, table_y, table_x, strength_ref, left_ref, spread_ref):
    high, low = two_terms(field)
    left_ref[0:CELLS, 0:COLS] = high
    left_ref[0:CELLS, COLS : 2 * COLS] = high
    left_ref[CELLS : 2 * CELLS, 0:COLS] = low
    left_ref[CELLS : 2 * CELLS, COLS : 2 * COLS] = low
    for block in range(BLOCKS):
        lanes = pl.ds(block * BLOCK, BLOCK)
        both = jnp.dot(left_ref[...], table_z[:, lanes], preferred_element_type=jnp.float32)
        sampled = (both[0:CELLS] + both[CELLS : 2 * CELLS]).reshape(PLANES, ROWS, BLOCK)
        along_y = table_y[:, lanes]
        along_x = table_x[:, lanes]
        total = jnp.zeros((8, BLOCK), jnp.float32)
        for plane in range(PLANES):
            summed = jnp.sum((sampled[plane] * along_y).reshape(ROWS // 8, 8, BLOCK), axis=0)
            total = total + summed * along_x[plane : plane + 1]
        values = jnp.sum(total, axis=0, keepdims=True) * strength_ref[0:1, lanes]
        for plane in range(PLANES):
            high, low = two_terms(along_y * (along_x[plane : plane + 1] * values))
            spread_ref[plane * ROWS : (plane + 1) * ROWS, lanes] = high
            spread_ref[CELLS + plane * ROWS : CELLS + (plane + 1) * ROWS, lanes] = low
    result = lax.dot_general(
        spread_ref[...], table_z[...], (((1,), (1,)), ((), ())), preferred_element_type=jnp.float32
    )
    result = result[0:CELLS] + result[CELLS : 2 * CELLS]
    return result[:, 0:COLS] + result[:, COLS : 2 * COLS]


MASS_TAPS = (1.0 / 120.0, 26.0 / 120.0, 66.0 / 120.0)
STIFF_TAPS = (-1.0 / 6.0, -1.0 / 3.0, 1.0)


def five(taps, values):
    return taps[2] * values[2] + taps[1] * (values[1] + values[3]) + taps[0] * (values[0] + values[4])


def own_part(taps, p):
    near, far = taps[1], taps[0]
    return [
        taps[2] * p[0] + near * p[1] + far * p[2],
        taps[2] * p[1] + near * (p[0] + p[2]) + far * p[3],
        taps[2] * p[2] + near * (p[1] + p[3]) + far * p[0],
        taps[2] * p[3] + near * p[2] + far * p[1],
    ]


def cross_part(taps, p):
    near, far = taps[1], taps[0]
    return [far * p[0] + near * p[1], far * p[1], far * p[2], near * p[2] + far * p[3]]


def outward_part(taps, p):
    near, far = taps[1], taps[0]
    return [far * p[0], near * p[0] + far * p[1], far * p[2] + near * p[3], far * p[3]]


def stencil(part, planes, stiff_ref, mass_ref):
    for k, (stiff_x, mass_x) in enumerate(zip(part(STIFF_TAPS, planes), part(MASS_TAPS, planes))):
        stiff_ref[k, EDGE : EDGE + ROWS, :] = stiff_x
        mass_ref[k, EDGE : EDGE + ROWS, :] = mass_x
    lane = lax.broadcasted_iota(jnp.int32, (ROWS, COLS), 1)

    def along_z(value):
        return [
            jnp.where(lane >= 2, pltpu.roll(value, 2, 1), 0.0),
            jnp.where(lane >= 1, pltpu.roll(value, 1, 1), 0.0),
            value,
            jnp.where(lane < COLS - 1, pltpu.roll(value, COLS - 1, 1), 0.0),
            jnp.where(lane < COLS - 2, pltpu.roll(value, COLS - 2, 1), 0.0),
        ]

    out = []
    for k in range(PLANES):
        stiff_x = [stiff_ref[k, EDGE - 2 + s : EDGE - 2 + s + ROWS, :] for s in range(5)]
        mass_x = [mass_ref[k, EDGE - 2 + s : EDGE - 2 + s + ROWS, :] for s in range(5)]
        mixed = five(MASS_TAPS, stiff_x) + five(STIFF_TAPS, mass_x)
        out.append(five(MASS_TAPS, along_z(mixed)) + five(STIFF_TAPS, along_z(five(MASS_TAPS, mass_x))))
    return out


def folded(moment, lanes):
    shift = COLS // 2
    while shift >= lanes:
        moment = moment + pltpu.roll(moment, shift, 1)
        shift //= 2
    return moment


def lane_groups():
    lane = lax.broadcasted_iota(jnp.int32, (1, COLS), 1)
    return [lane // 8 == 4, lane // 8 == 5, lane // 8 == 6, lane < 32]


def combine(rows):
    lane = lax.broadcasted_iota(jnp.int32, (1, COLS), 1)
    largest = jnp.max(rows, axis=0, keepdims=True)
    ratio = pltpu.roll(rows * (1.0 / largest), COLS // 2, 1)
    total = jnp.sum(rows * (ratio * ratio), axis=0, keepdims=True)
    return jnp.where(lane >= 64, largest, total)


def kernel(
    right_in, guess_in, cell_in, offset_in, weight_in, mask_in, count_ref,
    residual, image, second, out_factor,
    right_ref, cell_ref, offset_ref, weight_ref, mask_ref,
    guess, known, partial, outward, weighed, stiff_ref, mass_ref,
    table_z, table_y, table_x, strength_ref, left_ref, spread_ref,
    load_sem, halo_send, halo_recv, sum_send, sum_recv, entered, sums, *arrivals,
):
    here = coordinates()
    device = lax.axis_index("bricks") * 4 + lax.axis_index("pts")
    before, after = (device + 255) % 256, (device + 1) % 256
    left, right = (before // 4, before % 4), (after // 4, after % 4)
    peers = [stage_peers(here, axes) for axes in STAGES]

    barrier = pltpu.get_barrier_semaphore()
    lines = {axis: stage_peers(here, (axis,)) for axis in SIZES}
    greeted = [left, right] + lines["z"] + lines["y"] + lines["x"] + lines["core"]
    for peer in greeted[0:2]:
        pl.semaphore_signal(barrier, inc=1, device_id=peer, device_id_type=MESH)
    loads = [
        pltpu.make_async_copy(source, target, load_sem.at[k])
        for k, (source, target) in enumerate((
            (cell_in, cell_ref),
            (offset_in, offset_ref),
            (weight_in, weight_ref),
            (mask_in, mask_ref),
            (guess_in, guess.at[pl.ds(2, PLANES)]),
            (right_in, right_ref),
        ))
    ]
    for load in loads:
        load.start()
    for peer in greeted[2:]:
        pl.semaphore_signal(barrier, inc=1, device_id=peer, device_id_type=MESH)

    first, last = device == 0, device == 255
    for ref in (stiff_ref, mass_ref):
        ref[:, 0:EDGE, :] = jnp.zeros((PLANES, EDGE, COLS), jnp.float32)
        ref[:, EDGE + ROWS : 2 * EDGE + ROWS, :] = jnp.zeros((PLANES, EDGE, COLS), jnp.float32)
    for load in loads[0:4]:
        load.wait()
    build_tables(cell_ref, offset_ref, weight_ref, mask_ref, count_ref, table_z, table_y, table_x, strength_ref)
    tables = (table_z, table_y, table_x, strength_ref, left_ref, spread_ref)

    loads[4].wait()
    pl.semaphore_wait(barrier, len(greeted))
    started = []

    def send(field, turn):
        copies = []
        for side, (source, target) in enumerate(((2, 6), (4, 0))):
            copy = pltpu.make_async_remote_copy(
                src_ref=field.at[pl.ds(source, 2)],
                dst_ref=field.at[pl.ds(target, 2)],
                send_sem=halo_send.at[turn, side],
                recv_sem=halo_recv.at[turn, side],
                device_id=(left, right)[side],
                device_id_type=MESH,
            )
            copy.start()
            copies.append(copy)
        started.extend(copies)
        return copies

    def landed(copies):
        for copy in copies:
            copy.wait_recv()

    def screened(field):
        return screen(field.reshape(CELLS, COLS), *tables).reshape(PLANES, ROWS, COLS)

    def smooth(part, planes):
        return stencil(part, planes, stiff_ref, mass_ref)

    def four(ref, at):
        return [ref[at + k] for k in range(PLANES)]

    def beside(field, added):
        planes = [field[k] for k in (0, 1, 6, 7)]
        if added is not None:
            planes = [p + outward[k] for k, p in enumerate(planes)]
        return [jnp.where(first, 0.0, p) for p in planes[0:2]] + [jnp.where(last, 0.0, p) for p in planes[2:4]]

    def fold(value):
        return value.reshape(CELLS // 8, 8, COLS)

    def dot(a, b):
        return jnp.sum(fold(a) * fold(b), axis=0)

    copies = send(guess, 0)
    for peer in lines["y"]:
        pl.semaphore_signal(entered.at[0], inc=1, device_id=peer, device_id_type=MESH)
    own = smooth(own_part, four(guess, 2))
    loads[5].wait()
    for k in range(PLANES):
        known[2 + k] = right_ref[k] - own[k]
    known[2:6] = known[2:6] - screened(guess[2:6])
    edge = send(known, 1)
    added = smooth(outward_part, four(guess, 2))
    for k in range(PLANES):
        outward[k] = -added[k]

    landed(copies)
    added = smooth(cross_part, beside(guess, None))
    for k in range(PLANES):
        residual[k] = known[2 + k] - added[k]
    own = smooth(own_part, four(residual, 0))
    for k in range(PLANES):
        partial[2 + k] = own[k]
    partial[2:6] = partial[2:6] + screened(residual[...])
    copies = send(partial, 2)
    pl.semaphore_wait(entered.at[0], len(lines["y"]))
    for peer in lines["x"]:
        pl.semaphore_signal(entered.at[1], inc=1, device_id=peer, device_id_type=MESH)

    landed(edge)
    added = smooth(cross_part, beside(known, outward))
    for k in range(PLANES):
        image[k] = partial[2 + k] + added[k]
    added = smooth(outward_part, four(residual, 0))
    for k in range(PLANES):
        outward[k] = added[k]
    own = smooth(own_part, four(image, 0))
    for k in range(PLANES):
        second[k] = own[k]
    second[...] = second[...] + screened(image[...])

    scale = jnp.max(jnp.max(jnp.abs(fold(residual[...])), axis=0), axis=0, keepdims=True)
    scale = jnp.maximum(jnp.max(scale, axis=1, keepdims=True), 1e-30)
    inverse = 1.0 / scale
    r0 = residual[...] * inverse
    w = image[...] * inverse
    u = second[...] * inverse
    groups = lane_groups()
    row = jnp.where(lax.broadcasted_iota(jnp.int32, (1, COLS), 1) >= 64, scale, 0.0)
    for group, a, b in zip(groups, (r0, r0, w), (r0, w, w)):
        row = jnp.where(group, folded(jnp.sum(dot(a, b), axis=0, keepdims=True), 8), row)
    last_moment = dot(w, u)

    added = smooth(outward_part, four(image, 0))
    for k in range(PLANES):
        weighed[k] = added[k] * inverse

    landed(copies)
    halo = beside(partial, outward)
    for k in range(PLANES):
        last_moment = last_moment + jnp.sum(
            ((halo[k] * inverse) * weighed[k]).reshape(ROWS // 8, 8, COLS), axis=0
        )
    row = jnp.where(groups[3], folded(jnp.sum(last_moment, axis=0, keepdims=True), 32), row)
    pl.semaphore_wait(entered.at[1], len(lines["x"]))

    for turn, arrived in enumerate(arrivals):
        count = len(peers[turn])
        sums[turn] = row
        arrived[count : count + 1, :] = row
        for slot, peer in enumerate(peers[turn]):
            pltpu.make_async_remote_copy(
                src_ref=sums.at[turn],
                dst_ref=arrived.at[pl.ds(slot, 1)],
                send_sem=sum_send.at[turn],
                recv_sem=sum_recv.at[turn],
                device_id=peer,
                device_id_type=MESH,
            ).start()
        if turn == len(STAGES) - 1:
            added = smooth(cross_part, beside(partial, outward))
            for k in range(PLANES):
                second[k] = second[k] + added[k]
        whole = arrived.at[pl.ds(0, count)]
        pltpu.make_async_copy(whole, whole, sum_recv.at[turn]).wait()
        row = combine(arrived[...])

    m0, m1, m2, m3 = (jnp.sum(jnp.where(group, row, 0.0), axis=1, keepdims=True) for group in groups)
    a0 = m0 / m1
    g = a0 * (m2 / m1)
    a1 = (g - 1.0) * m1 / (a0 * m3 - g * m2)
    c1 = a0 + a1 * g
    c2 = a1 * a0
    out_factor[...] = jnp.concatenate([jnp.broadcast_to(c, (1, COLS)) for c in (c1, c2)] * 4, axis=0)

    for copy in started:
        copy.wait_send()
    for turn, arrived in enumerate(arrivals):
        whole = arrived.at[pl.ds(0, len(peers[turn]))]
        pltpu.make_async_copy(whole, whole, sum_send.at[turn]).wait()


def body(right_side, initial_guess, point_cell, point_offset, point_weight, point_mask, block_count):
    slab = pltpu.VMEM((PLANES, ROWS, COLS), jnp.float32)
    vmem = pl.BlockSpec(memory_space=pltpu.VMEM)
    groups = []
    for axes in STAGES:
        size = 1
        for axis in axes:
            size *= SIZES[axis]
        groups.append(size)
    r0, w, u, factor = pl.pallas_call(
        kernel,
        out_shape=(slab, slab, slab, pltpu.VMEM((8, COLS), jnp.float32)),
        in_specs=[pl.BlockSpec(memory_space=pltpu.HBM)] * 6 + [vmem],
        out_specs=(vmem,) * 4,
        scratch_shapes=[
            pltpu.VMEM((PLANES, ROWS, COLS), jnp.float32),
            pltpu.VMEM((3, POINTS), jnp.int32),
            pltpu.VMEM((3, POINTS), jnp.float32),
            pltpu.VMEM((POINTS // COLS, COLS), jnp.float32),
            pltpu.VMEM((POINTS // COLS, COLS), jnp.int32),
            pltpu.VMEM((PLANES + 4, ROWS, COLS), jnp.float32),
            pltpu.VMEM((PLANES + 4, ROWS, COLS), jnp.float32),
            pltpu.VMEM((PLANES + 4, ROWS, COLS), jnp.float32),
            pltpu.VMEM((PLANES, ROWS, COLS), jnp.float32),
            pltpu.VMEM((PLANES, ROWS, COLS), jnp.float32),
            pltpu.VMEM((PLANES, ROWS + 2 * EDGE, COLS), jnp.float32),
            pltpu.VMEM((PLANES, ROWS + 2 * EDGE, COLS), jnp.float32),
            pltpu.VMEM((2 * COLS, POINTS), jnp.bfloat16),
            pltpu.VMEM((ROWS, POINTS), jnp.float32),
            pltpu.VMEM((8, POINTS), jnp.float32),
            pltpu.VMEM((8, POINTS), jnp.float32),
            pltpu.VMEM((2 * CELLS, 2 * COLS), jnp.bfloat16),
            pltpu.VMEM((2 * CELLS, POINTS), jnp.bfloat16),
            pltpu.SemaphoreType.DMA((6,)),
            pltpu.SemaphoreType.DMA((3, 2)),
            pltpu.SemaphoreType.DMA((3, 2)),
            pltpu.SemaphoreType.DMA((len(STAGES),)),
            pltpu.SemaphoreType.DMA((len(STAGES),)),
            pltpu.SemaphoreType.REGULAR((2,)),
            pltpu.VMEM((len(STAGES), 1, COLS), jnp.float32),
        ]
        + [pltpu.VMEM((size, COLS), jnp.float32) for size in groups],
        compiler_params=pltpu.CompilerParams(
            collective_id=0, has_side_effects=True, vmem_limit_bytes=56 * 1024 * 1024
        ),
        cost_estimate=pl.CostEstimate(flops=3_000_000_000, bytes_accessed=700_000, transcendentals=0),
    )(
        right_side, initial_guess, point_cell, point_offset,
        point_weight.reshape(POINTS // COLS, COLS), point_mask.reshape(POINTS // COLS, COLS), block_count.reshape(1, 1),
    )
    c1, c2 = factor[0], factor[1]
    return initial_guess + c1 * r0 - c2 * w, r0 - c1 * w + c2 * u


def solution(mesh):
    placed = (
        P(("bricks", "pts"), None, None),
        P(("bricks", "pts"), None, None),
        P(None, ("bricks", "pts")),
        P(None, ("bricks", "pts")),
        P(("bricks", "pts")),
        P(("bricks", "pts")),
        P(("bricks", "pts")),
    )
    return jax.shard_map(
        body,
        mesh=mesh,
        in_specs=placed,
        out_specs=(P(("bricks", "pts"), None, None), P(("bricks", "pts"), None, None)),
        check_vma=False,
    )
```

```python
import functools

import jax
import jax.numpy as jnp
from jax import lax
from jax.experimental import pallas as pl
from jax.experimental.pallas import tpu as pltpu
from jax.sharding import PartitionSpec as P

MESH = pl.DeviceIdType.MESH

PLANES = 4
ROWS = 64
COLS = 128
CELLS = PLANES * ROWS
BLOCK = 256
BLOCKS = 8
POINTS = BLOCK * BLOCKS
EDGE = 8

SIZES = {"x": 4, "y": 4, "z": 8, "core": 2}
STAGES = (("core",), ("x", "y", "z"))


def spline_weights(offset):
    return (0.5 * (0.5 - offset) ** 2, 0.75 - offset * offset, 0.5 * (0.5 + offset) ** 2)


def coordinates():
    brick = lax.axis_index("bricks")
    return {
        "x": lax.axis_index("pts"),
        "y": brick // 16,
        "z": (brick // 2) % 8,
        "core": brick % 2,
    }


def device_of(place):
    return ((place["y"] * 8 + place["z"]) * 2 + place["core"], place["x"])


def stage_peers(here, axes):
    steps = [{}]
    for axis in axes:
        steps = [dict(step, **{axis: k}) for step in steps for k in range(SIZES[axis])]
    peers = []
    far = lambda step: sum(min(k, SIZES[axis] - k) for axis, k in step.items())
    for step in sorted(steps[1:], key=far, reverse=True):
        place = dict(here)
        for axis, k in step.items():
            if k:
                place[axis] = (here[axis] + k) % SIZES[axis]
        peers.append(device_of(place))
    return peers


def two_terms(value):
    high = value.astype(jnp.bfloat16)
    low = (value - high.astype(jnp.float32)).astype(jnp.bfloat16)
    return high, low


def block_row(ref, block):
    return jnp.concatenate([ref[2 * block : 2 * block + 1, :], ref[2 * block + 1 : 2 * block + 2, :]], axis=1)


def build_tables(cell_ref, offset_ref, weight_ref, mask_ref, count_ref, table_z, table_y, table_x, strength_ref):
    count = count_ref[0:1, 0:1]
    for block in range(BLOCKS):
        lanes = pl.ds(block * BLOCK, BLOCK)

        def factors(axis):
            return cell_ref[axis : axis + 1, lanes], spline_weights(offset_ref[axis : axis + 1, lanes])

        def spread_out(cell, rows, parts):
            apart = lax.broadcasted_iota(jnp.int32, (rows, BLOCK), 0) - cell
            zero = jnp.zeros((rows, BLOCK), jnp.float32)
            before, at, after = apart == -1, apart == 0, apart == 1
            return [jnp.where(before, a, jnp.where(at, b, jnp.where(after, c, zero))) for a, b, c in parts]

        cell, parts = factors(2)
        terms = [two_terms(part) for part in parts]
        high, low = spread_out(
            cell,
            COLS,
            [[t[0].astype(jnp.float32) for t in terms], [t[1].astype(jnp.float32) for t in terms]],
        )
        table_z[0:COLS, lanes] = high.astype(jnp.bfloat16)
        table_z[COLS : 2 * COLS, lanes] = low.astype(jnp.bfloat16)
        cell, parts = factors(1)
        table_y[:, lanes] = spread_out(cell, ROWS, [parts])[0]
        cell, parts = factors(0)
        table_x[:, lanes] = spread_out(cell, 8, [parts])[0]
        alive = jnp.where(count > block, 1.0, 0.0)
        strength_ref[0:1, lanes] = (
            jnp.where(block_row(mask_ref, block) == 1, block_row(weight_ref, block), 0.0) * alive
        )


def sample(field, table_z, table_y, table_x, strength_ref, left_ref, spread_ref):
    high, low = two_terms(field)
    left_ref[0:CELLS, 0:COLS] = high
    left_ref[0:CELLS, COLS : 2 * COLS] = high
    left_ref[CELLS : 2 * CELLS, 0:COLS] = low
    left_ref[CELLS : 2 * CELLS, COLS : 2 * COLS] = low
    for block in range(BLOCKS):
        lanes = pl.ds(block * BLOCK, BLOCK)
        both = jnp.dot(left_ref[...], table_z[:, lanes], preferred_element_type=jnp.float32)
        sampled = (both[0:CELLS] + both[CELLS : 2 * CELLS]).reshape(PLANES, ROWS, BLOCK)
        along_y = table_y[:, lanes]
        along_x = table_x[:, lanes]
        total = jnp.zeros((8, BLOCK), jnp.float32)
        for plane in range(PLANES):
            summed = jnp.sum((sampled[plane] * along_y).reshape(ROWS // 8, 8, BLOCK), axis=0)
            total = total + summed * along_x[plane : plane + 1]
        values = jnp.sum(total, axis=0, keepdims=True) * strength_ref[0:1, lanes]
        for plane in range(PLANES):
            high, low = two_terms(along_y * (along_x[plane : plane + 1] * values))
            spread_ref[plane * ROWS : (plane + 1) * ROWS, lanes] = high
            spread_ref[CELLS + plane * ROWS : CELLS + (plane + 1) * ROWS, lanes] = low


def gathered(table_z, spread_ref):
    result = lax.dot_general(
        spread_ref[...], table_z[...], (((1,), (1,)), ((), ())), preferred_element_type=jnp.float32
    )
    result = result[0:CELLS] + result[CELLS : 2 * CELLS]
    return result[:, 0:COLS] + result[:, COLS : 2 * COLS]


MASS_TAPS = (1.0 / 120.0, 26.0 / 120.0, 66.0 / 120.0)
STIFF_TAPS = (-1.0 / 6.0, -1.0 / 3.0, 1.0)


def five(taps, values):
    return taps[2] * values[2] + taps[1] * (values[1] + values[3]) + taps[0] * (values[0] + values[4])


def own_part(taps, p):
    near, far = taps[1], taps[0]
    return [
        taps[2] * p[0] + near * p[1] + far * p[2],
        taps[2] * p[1] + near * (p[0] + p[2]) + far * p[3],
        taps[2] * p[2] + near * (p[1] + p[3]) + far * p[0],
        taps[2] * p[3] + near * p[2] + far * p[1],
    ]


def cross_part(taps, p):
    near, far = taps[1], taps[0]
    return [far * p[0] + near * p[1], far * p[1], far * p[2], near * p[2] + far * p[3]]


def outward_part(taps, p):
    near, far = taps[1], taps[0]
    return [far * p[0], near * p[0] + far * p[1], far * p[2] + near * p[3], far * p[3]]


def stencil(part, planes, stiff_ref, mass_ref):
    for k, (stiff_x, mass_x) in enumerate(zip(part(STIFF_TAPS, planes), part(MASS_TAPS, planes))):
        stiff_ref[k, EDGE : EDGE + ROWS, :] = stiff_x
        mass_ref[k, EDGE : EDGE + ROWS, :] = mass_x
    lane = lax.broadcasted_iota(jnp.int32, (ROWS, COLS), 1)

    def along_z(value):
        return [
            jnp.where(lane >= 2, pltpu.roll(value, 2, 1), 0.0),
            jnp.where(lane >= 1, pltpu.roll(value, 1, 1), 0.0),
            value,
            jnp.where(lane < COLS - 1, pltpu.roll(value, COLS - 1, 1), 0.0),
            jnp.where(lane < COLS - 2, pltpu.roll(value, COLS - 2, 1), 0.0),
        ]

    out = []
    for k in range(PLANES):
        stiff_x = [stiff_ref[k, EDGE - 2 + s : EDGE - 2 + s + ROWS, :] for s in range(5)]
        mass_x = [mass_ref[k, EDGE - 2 + s : EDGE - 2 + s + ROWS, :] for s in range(5)]
        mixed = five(MASS_TAPS, stiff_x) + five(STIFF_TAPS, mass_x)
        out.append(five(MASS_TAPS, along_z(mixed)) + five(STIFF_TAPS, along_z(five(MASS_TAPS, mass_x))))
    return out


def folded(moment, lanes):
    shift = COLS // 2
    while shift >= lanes:
        moment = moment + pltpu.roll(moment, shift, 1)
        shift //= 2
    return moment


def lane_groups():
    lane = lax.broadcasted_iota(jnp.int32, (1, COLS), 1)
    return [lane // 8 == 4, lane // 8 == 5, lane // 8 == 6, lane < 32]


def combine(rows):
    lane = lax.broadcasted_iota(jnp.int32, (1, COLS), 1)
    largest = jnp.max(rows, axis=0, keepdims=True)
    ratio = pltpu.roll(rows * (1.0 / largest), COLS // 2, 1)
    total = jnp.sum(rows * (ratio * ratio), axis=0, keepdims=True)
    return jnp.where(lane >= 64, largest, total)


def kernel(
    right_in, guess_in, cell_in, offset_in, weight_in, mask_in, count_ref,
    residual, image, second, out_factor,
    right_ref, cell_ref, offset_ref, weight_ref, mask_ref,
    guess, known, partial, outward, weighed, stiff_ref, mass_ref,
    table_z, table_y, table_x, strength_ref, left_ref, spread_ref,
    load_sem, halo_send, halo_recv, sum_send, sum_recv, entered, sums, *arrivals,
):
    here = coordinates()
    device = lax.axis_index("bricks") * 4 + lax.axis_index("pts")
    before, after = (device + 255) % 256, (device + 1) % 256
    left, right = (before // 4, before % 4), (after // 4, after % 4)
    peers = [stage_peers(here, axes) for axes in STAGES]

    barrier = pltpu.get_barrier_semaphore()
    lines = {axis: stage_peers(here, (axis,)) for axis in SIZES}
    greeted = [left, right] + lines["z"] + lines["y"] + lines["x"] + lines["core"]
    for peer in greeted[0:2]:
        pl.semaphore_signal(barrier, inc=1, device_id=peer, device_id_type=MESH)
    for peer in greeted[2:]:
        pl.semaphore_signal(barrier, inc=1, device_id=peer, device_id_type=MESH)
    loads = [
        pltpu.make_async_copy(source, target, load_sem.at[k])
        for k, (source, target) in enumerate((
            (cell_in, cell_ref),
            (offset_in, offset_ref),
            (weight_in, weight_ref),
            (mask_in, mask_ref),
            (guess_in, guess.at[pl.ds(2, PLANES)]),
            (right_in, right_ref),
        ))
    ]
    for load in loads:
        load.start()

    first, last = device == 0, device == 255
    for ref in (stiff_ref, mass_ref):
        ref[:, 0:EDGE, :] = jnp.zeros((PLANES, EDGE, COLS), jnp.float32)
        ref[:, EDGE + ROWS : 2 * EDGE + ROWS, :] = jnp.zeros((PLANES, EDGE, COLS), jnp.float32)
    loads[4].wait()
    pl.semaphore_wait(barrier, len(greeted))
    started = []

    def send(field, turn):
        copies = []
        for side, (source, target) in enumerate(((2, 6), (4, 0))):
            copy = pltpu.make_async_remote_copy(
                src_ref=field.at[pl.ds(source, 2)],
                dst_ref=field.at[pl.ds(target, 2)],
                send_sem=halo_send.at[turn, side],
                recv_sem=halo_recv.at[turn, side],
                device_id=(left, right)[side],
                device_id_type=MESH,
            )
            copy.start()
            copies.append(copy)
        started.extend(copies)
        return copies

    def landed(copies):
        for copy in copies:
            copy.wait_recv()

    def screened(field):
        sample(field.reshape(CELLS, COLS), *tables)
        return gathered(table_z, spread_ref).reshape(PLANES, ROWS, COLS)

    def smooth(part, planes):
        return stencil(part, planes, stiff_ref, mass_ref)

    def four(ref, at):
        return [ref[at + k] for k in range(PLANES)]

    def beside(field, added):
        planes = [field[k] for k in (0, 1, 6, 7)]
        if added is not None:
            planes = [p + outward[k] for k, p in enumerate(planes)]
        return [jnp.where(first, 0.0, p) for p in planes[0:2]] + [jnp.where(last, 0.0, p) for p in planes[2:4]]

    def fold(value):
        return value.reshape(CELLS // 8, 8, COLS)

    def dot(a, b):
        return jnp.sum(fold(a) * fold(b), axis=0)

    copies = send(guess, 0)
    for peer in lines["y"]:
        pl.semaphore_signal(entered.at[0], inc=1, device_id=peer, device_id_type=MESH)
    for load in loads[0:4]:
        load.wait()
    build_tables(cell_ref, offset_ref, weight_ref, mask_ref, count_ref, table_z, table_y, table_x, strength_ref)
    tables = (table_z, table_y, table_x, strength_ref, left_ref, spread_ref)

    own = smooth(own_part, four(guess, 2))
    loads[5].wait()
    for k in range(PLANES):
        known[2 + k] = right_ref[k] - own[k]
    known[2:6] = known[2:6] - screened(guess[2:6])
    edge = send(known, 1)
    added = smooth(outward_part, four(guess, 2))
    for k in range(PLANES):
        outward[k] = -added[k]

    landed(copies)
    added = smooth(cross_part, beside(guess, None))
    for k in range(PLANES):
        residual[k] = known[2 + k] - added[k]
    sample(residual[...].reshape(CELLS, COLS), *tables)
    spread = gathered(table_z, spread_ref)
    own = smooth(own_part, four(residual, 0))
    for k in range(PLANES):
        partial[2 + k] = own[k] + spread[k * ROWS : (k + 1) * ROWS]
    copies = send(partial, 2)
    pl.semaphore_wait(entered.at[0], len(lines["y"]))
    for peer in lines["x"]:
        pl.semaphore_signal(entered.at[1], inc=1, device_id=peer, device_id_type=MESH)

    landed(edge)
    added = smooth(cross_part, beside(known, outward))
    for k in range(PLANES):
        image[k] = partial[2 + k] + added[k]
    added = smooth(outward_part, four(residual, 0))
    for k in range(PLANES):
        outward[k] = added[k]
    own = smooth(own_part, four(image, 0))
    for k in range(PLANES):
        second[k] = own[k]
    second[...] = second[...] + screened(image[...])

    scale = jnp.max(jnp.max(jnp.abs(fold(residual[...])), axis=0), axis=0, keepdims=True)
    scale = jnp.maximum(jnp.max(scale, axis=1, keepdims=True), 1e-30)
    inverse = 1.0 / scale
    r0 = residual[...] * inverse
    w = image[...] * inverse
    u = second[...] * inverse
    groups = lane_groups()
    row = jnp.where(lax.broadcasted_iota(jnp.int32, (1, COLS), 1) >= 64, scale, 0.0)
    for group, a, b in zip(groups, (r0, r0, w), (r0, w, w)):
        row = jnp.where(group, folded(jnp.sum(dot(a, b), axis=0, keepdims=True), 8), row)
    last_moment = dot(w, u)

    added = smooth(outward_part, four(image, 0))
    for k in range(PLANES):
        weighed[k] = added[k] * inverse

    landed(copies)
    halo = beside(partial, outward)
    for k in range(PLANES):
        last_moment = last_moment + jnp.sum(
            ((halo[k] * inverse) * weighed[k]).reshape(ROWS // 8, 8, COLS), axis=0
        )
    row = jnp.where(groups[3], folded(jnp.sum(last_moment, axis=0, keepdims=True), 32), row)
    pl.semaphore_wait(entered.at[1], len(lines["x"]))

    for turn, arrived in enumerate(arrivals):
        count = len(peers[turn])
        sums[turn] = row
        arrived[count : count + 1, :] = row
        for slot, peer in enumerate(peers[turn]):
            pltpu.make_async_remote_copy(
                src_ref=sums.at[turn],
                dst_ref=arrived.at[pl.ds(slot, 1)],
                send_sem=sum_send.at[turn],
                recv_sem=sum_recv.at[turn],
                device_id=peer,
                device_id_type=MESH,
            ).start()
        if turn == len(STAGES) - 1:
            added = smooth(cross_part, beside(partial, outward))
            for k in range(PLANES):
                second[k] = second[k] + added[k]
        whole = arrived.at[pl.ds(0, count)]
        pltpu.make_async_copy(whole, whole, sum_recv.at[turn]).wait()
        row = combine(arrived[...])

    m0, m1, m2, m3 = (jnp.sum(jnp.where(group, row, 0.0), axis=1, keepdims=True) for group in groups)
    a0 = m0 / m1
    g = a0 * (m2 / m1)
    a1 = (g - 1.0) * m1 / (a0 * m3 - g * m2)
    c1 = a0 + a1 * g
    c2 = a1 * a0
    out_factor[...] = jnp.concatenate([jnp.broadcast_to(c, (1, COLS)) for c in (c1, c2)] * 4, axis=0)

    for copy in started:
        copy.wait_send()
    for turn, arrived in enumerate(arrivals):
        whole = arrived.at[pl.ds(0, len(peers[turn]))]
        pltpu.make_async_copy(whole, whole, sum_send.at[turn]).wait()


def body(right_side, initial_guess, point_cell, point_offset, point_weight, point_mask, block_count):
    slab = pltpu.VMEM((PLANES, ROWS, COLS), jnp.float32)
    vmem = pl.BlockSpec(memory_space=pltpu.VMEM)
    groups = []
    for axes in STAGES:
        size = 1
        for axis in axes:
            size *= SIZES[axis]
        groups.append(size)
    r0, w, u, factor = pl.pallas_call(
        kernel,
        out_shape=(slab, slab, slab, pltpu.VMEM((8, COLS), jnp.float32)),
        in_specs=[pl.BlockSpec(memory_space=pltpu.HBM)] * 6 + [vmem],
        out_specs=(vmem,) * 4,
        scratch_shapes=[
            pltpu.VMEM((PLANES, ROWS, COLS), jnp.float32),
            pltpu.VMEM((3, POINTS), jnp.int32),
            pltpu.VMEM((3, POINTS), jnp.float32),
            pltpu.VMEM((POINTS // COLS, COLS), jnp.float32),
            pltpu.VMEM((POINTS // COLS, COLS), jnp.int32),
            pltpu.VMEM((PLANES + 4, ROWS, COLS), jnp.float32),
            pltpu.VMEM((PLANES + 4, ROWS, COLS), jnp.float32),
            pltpu.VMEM((PLANES + 4, ROWS, COLS), jnp.float32),
            pltpu.VMEM((PLANES, ROWS, COLS), jnp.float32),
            pltpu.VMEM((PLANES, ROWS, COLS), jnp.float32),
            pltpu.VMEM((PLANES, ROWS + 2 * EDGE, COLS), jnp.float32),
            pltpu.VMEM((PLANES, ROWS + 2 * EDGE, COLS), jnp.float32),
            pltpu.VMEM((2 * COLS, POINTS), jnp.bfloat16),
            pltpu.VMEM((ROWS, POINTS), jnp.float32),
            pltpu.VMEM((8, POINTS), jnp.float32),
            pltpu.VMEM((8, POINTS), jnp.float32),
            pltpu.VMEM((2 * CELLS, 2 * COLS), jnp.bfloat16),
            pltpu.VMEM((2 * CELLS, POINTS), jnp.bfloat16),
            pltpu.SemaphoreType.DMA((6,)),
            pltpu.SemaphoreType.DMA((3, 2)),
            pltpu.SemaphoreType.DMA((3, 2)),
            pltpu.SemaphoreType.DMA((len(STAGES),)),
            pltpu.SemaphoreType.DMA((len(STAGES),)),
            pltpu.SemaphoreType.REGULAR((2,)),
            pltpu.VMEM((len(STAGES), 1, COLS), jnp.float32),
        ]
        + [pltpu.VMEM((size, COLS), jnp.float32) for size in groups],
        compiler_params=pltpu.CompilerParams(
            collective_id=0, has_side_effects=True, vmem_limit_bytes=56 * 1024 * 1024
        ),
        cost_estimate=pl.CostEstimate(flops=3_000_000_000, bytes_accessed=700_000, transcendentals=0),
    )(
        right_side, initial_guess, point_cell, point_offset,
        point_weight.reshape(POINTS // COLS, COLS), point_mask.reshape(POINTS // COLS, COLS), block_count.reshape(1, 1),
    )
    c1, c2 = factor[0], factor[1]
    return initial_guess + c1 * r0 - c2 * w, r0 - c1 * w + c2 * u


def solution(mesh):
    placed = (
        P(("bricks", "pts"), None, None),
        P(("bricks", "pts"), None, None),
        P(None, ("bricks", "pts")),
        P(None, ("bricks", "pts")),
        P(("bricks", "pts")),
        P(("bricks", "pts")),
        P(("bricks", "pts")),
    )
    return jax.shard_map(
        body,
        mesh=mesh,
        in_specs=placed,
        out_specs=(P(("bricks", "pts"), None, None), P(("bricks", "pts"), None, None)),
        check_vma=False,
    )
```

```python
import functools

import jax
import jax.numpy as jnp
from jax import lax
from jax.experimental import pallas as pl
from jax.experimental.pallas import tpu as pltpu
from jax.sharding import PartitionSpec as P

MESH = pl.DeviceIdType.MESH

PLANES = 4
ROWS = 64
COLS = 128
CELLS = PLANES * ROWS
BLOCK = 256
BLOCKS = 8
POINTS = BLOCK * BLOCKS
EDGE = 8

SIZES = {"x": 4, "y": 4, "z": 8, "core": 2}
STAGES = (("core",), ("x", "y", "z"))


def spline_weights(offset):
    return (0.5 * (0.5 - offset) ** 2, 0.75 - offset * offset, 0.5 * (0.5 + offset) ** 2)


def coordinates():
    brick = lax.axis_index("bricks")
    return {
        "x": lax.axis_index("pts"),
        "y": brick // 16,
        "z": (brick // 2) % 8,
        "core": brick % 2,
    }


def device_of(place):
    return ((place["y"] * 8 + place["z"]) * 2 + place["core"], place["x"])


def stage_peers(here, axes):
    steps = [{}]
    for axis in axes:
        steps = [dict(step, **{axis: k}) for step in steps for k in range(SIZES[axis])]
    peers = []
    far = lambda step: sum(min(k, SIZES[axis] - k) for axis, k in step.items())
    for step in sorted(steps[1:], key=far, reverse=True):
        place = dict(here)
        for axis, k in step.items():
            if k:
                place[axis] = (here[axis] + k) % SIZES[axis]
        peers.append(device_of(place))
    return peers


def two_terms(value):
    high = value.astype(jnp.bfloat16)
    low = (value - high.astype(jnp.float32)).astype(jnp.bfloat16)
    return high, low


def block_row(ref, block):
    return jnp.concatenate([ref[2 * block : 2 * block + 1, :], ref[2 * block + 1 : 2 * block + 2, :]], axis=1)


def build_tables(cell_ref, offset_ref, weight_ref, mask_ref, count_ref, table_z, table_y, table_x, strength_ref):
    count = count_ref[0:1, 0:1]
    for block in range(BLOCKS):
        lanes = pl.ds(block * BLOCK, BLOCK)

        def factors(axis):
            return cell_ref[axis : axis + 1, lanes], spline_weights(offset_ref[axis : axis + 1, lanes])

        def spread_out(cell, rows, parts):
            apart = lax.broadcasted_iota(jnp.int32, (rows, BLOCK), 0) - cell
            zero = jnp.zeros((rows, BLOCK), jnp.float32)
            before, at, after = apart == -1, apart == 0, apart == 1
            return [jnp.where(before, a, jnp.where(at, b, jnp.where(after, c, zero))) for a, b, c in parts]

        cell, parts = factors(2)
        terms = [two_terms(part) for part in parts]
        high, low = spread_out(
            cell,
            COLS,
            [[t[0].astype(jnp.float32) for t in terms], [t[1].astype(jnp.float32) for t in terms]],
        )
        table_z[0:COLS, lanes] = high.astype(jnp.bfloat16)
        table_z[COLS : 2 * COLS, lanes] = low.astype(jnp.bfloat16)
        cell, parts = factors(1)
        table_y[:, lanes] = spread_out(cell, ROWS, [parts])[0]
        cell, parts = factors(0)
        table_x[:, lanes] = spread_out(cell, 8, [parts])[0]
        alive = jnp.where(count > block, 1.0, 0.0)
        strength_ref[0:1, lanes] = (
            jnp.where(block_row(mask_ref, block) == 1, block_row(weight_ref, block), 0.0) * alive
        )


def screen(field, table_z, table_y, table_x, strength_ref, left_ref, spread_ref):
    high, low = two_terms(field)
    left_ref[0:CELLS, 0:COLS] = high
    left_ref[0:CELLS, COLS : 2 * COLS] = high
    left_ref[CELLS : 2 * CELLS, 0:COLS] = low
    left_ref[CELLS : 2 * CELLS, COLS : 2 * COLS] = low
    for block in range(BLOCKS):
        lanes = pl.ds(block * BLOCK, BLOCK)
        both = jnp.dot(left_ref[...], table_z[:, lanes], preferred_element_type=jnp.float32)
        sampled = (both[0:CELLS] + both[CELLS : 2 * CELLS]).reshape(PLANES, ROWS, BLOCK)
        along_y = table_y[:, lanes]
        along_x = table_x[:, lanes]
        total = jnp.zeros((8, BLOCK), jnp.float32)
        for plane in range(PLANES):
            summed = jnp.sum((sampled[plane] * along_y).reshape(ROWS // 8, 8, BLOCK), axis=0)
            total = total + summed * along_x[plane : plane + 1]
        values = jnp.sum(total, axis=0, keepdims=True) * strength_ref[0:1, lanes]
        for plane in range(PLANES):
            high, low = two_terms(along_y * (along_x[plane : plane + 1] * values))
            spread_ref[plane * ROWS : (plane + 1) * ROWS, lanes] = high
            spread_ref[CELLS + plane * ROWS : CELLS + (plane + 1) * ROWS, lanes] = low
    result = lax.dot_general(
        spread_ref[...], table_z[...], (((1,), (1,)), ((), ())), preferred_element_type=jnp.float32
    )
    result = result[0:CELLS] + result[CELLS : 2 * CELLS]
    return result[:, 0:COLS] + result[:, COLS : 2 * COLS]


MASS_TAPS = (1.0 / 120.0, 26.0 / 120.0, 66.0 / 120.0)
STIFF_TAPS = (-1.0 / 6.0, -1.0 / 3.0, 1.0)


def five(taps, values):
    return taps[2] * values[2] + taps[1] * (values[1] + values[3]) + taps[0] * (values[0] + values[4])


def own_part(taps, p):
    near, far = taps[1], taps[0]
    return [
        taps[2] * p[0] + near * p[1] + far * p[2],
        taps[2] * p[1] + near * (p[0] + p[2]) + far * p[3],
        taps[2] * p[2] + near * (p[1] + p[3]) + far * p[0],
        taps[2] * p[3] + near * p[2] + far * p[1],
    ]


def cross_part(taps, p):
    near, far = taps[1], taps[0]
    return [far * p[0] + near * p[1], far * p[1], far * p[2], near * p[2] + far * p[3]]


def outward_part(taps, p):
    near, far = taps[1], taps[0]
    return [far * p[0], near * p[0] + far * p[1], far * p[2] + near * p[3], far * p[3]]


def stencil(part, planes, stiff_ref, mass_ref):
    for k, (stiff_x, mass_x) in enumerate(zip(part(STIFF_TAPS, planes), part(MASS_TAPS, planes))):
        stiff_ref[k, EDGE : EDGE + ROWS, :] = stiff_x
        mass_ref[k, EDGE : EDGE + ROWS, :] = mass_x
    lane = lax.broadcasted_iota(jnp.int32, (ROWS, COLS), 1)

    def along_z(value):
        return [
            jnp.where(lane >= 2, pltpu.roll(value, 2, 1), 0.0),
            jnp.where(lane >= 1, pltpu.roll(value, 1, 1), 0.0),
            value,
            jnp.where(lane < COLS - 1, pltpu.roll(value, COLS - 1, 1), 0.0),
            jnp.where(lane < COLS - 2, pltpu.roll(value, COLS - 2, 1), 0.0),
        ]

    out = []
    for k in range(PLANES):
        stiff_x = [stiff_ref[k, EDGE - 2 + s : EDGE - 2 + s + ROWS, :] for s in range(5)]
        mass_x = [mass_ref[k, EDGE - 2 + s : EDGE - 2 + s + ROWS, :] for s in range(5)]
        mixed = five(MASS_TAPS, stiff_x) + five(STIFF_TAPS, mass_x)
        out.append(five(MASS_TAPS, along_z(mixed)) + five(STIFF_TAPS, along_z(five(MASS_TAPS, mass_x))))
    return out


def folded(moment, lanes):
    shift = COLS // 2
    while shift >= lanes:
        moment = moment + pltpu.roll(moment, shift, 1)
        shift //= 2
    return moment


def lane_groups():
    lane = lax.broadcasted_iota(jnp.int32, (1, COLS), 1)
    return [lane // 8 == 4, lane // 8 == 5, lane // 8 == 6, lane < 32]


def combine(rows):
    lane = lax.broadcasted_iota(jnp.int32, (1, COLS), 1)
    largest = jnp.max(rows, axis=0, keepdims=True)
    ratio = pltpu.roll(rows * (1.0 / largest), COLS // 2, 1)
    total = jnp.sum(rows * (ratio * ratio), axis=0, keepdims=True)
    return jnp.where(lane >= 64, largest, total)


def kernel(
    right_in, guess_in, cell_in, offset_in, weight_in, mask_in, count_ref,
    residual, image, second, out_first, out_second,
    right_ref, cell_ref, offset_ref, weight_ref, mask_ref,
    guess, known, partial, outward, weighed, stiff_ref, mass_ref,
    table_z, table_y, table_x, strength_ref, left_ref, spread_ref,
    load_sem, halo_send, halo_recv, sum_send, sum_recv, entered, sums, *arrivals,
):
    here = coordinates()
    device = lax.axis_index("bricks") * 4 + lax.axis_index("pts")
    before, after = (device + 255) % 256, (device + 1) % 256
    left, right = (before // 4, before % 4), (after // 4, after % 4)
    peers = [stage_peers(here, axes) for axes in STAGES]

    barrier = pltpu.get_barrier_semaphore()
    lines = {axis: stage_peers(here, (axis,)) for axis in SIZES}
    greeted = [left, right] + lines["z"] + lines["y"] + lines["x"] + lines["core"]
    for peer in greeted[0:2]:
        pl.semaphore_signal(barrier, inc=1, device_id=peer, device_id_type=MESH)
    loads = [
        pltpu.make_async_copy(source, target, load_sem.at[k])
        for k, (source, target) in enumerate((
            (cell_in, cell_ref),
            (offset_in, offset_ref),
            (weight_in, weight_ref),
            (mask_in, mask_ref),
            (guess_in, guess.at[pl.ds(2, PLANES)]),
            (right_in, right_ref),
        ))
    ]
    for load in loads:
        load.start()
    for peer in greeted[2:]:
        pl.semaphore_signal(barrier, inc=1, device_id=peer, device_id_type=MESH)

    first, last = device == 0, device == 255
    for ref in (stiff_ref, mass_ref):
        ref[:, 0:EDGE, :] = jnp.zeros((PLANES, EDGE, COLS), jnp.float32)
        ref[:, EDGE + ROWS : 2 * EDGE + ROWS, :] = jnp.zeros((PLANES, EDGE, COLS), jnp.float32)
    for load in loads[0:4]:
        load.wait()
    build_tables(cell_ref, offset_ref, weight_ref, mask_ref, count_ref, table_z, table_y, table_x, strength_ref)
    tables = (table_z, table_y, table_x, strength_ref, left_ref, spread_ref)

    loads[4].wait()
    pl.semaphore_wait(barrier, len(greeted))
    started = []

    def send(field, turn):
        copies = []
        for side, (source, target) in enumerate(((2, 6), (4, 0))):
            copy = pltpu.make_async_remote_copy(
                src_ref=field.at[pl.ds(source, 2)],
                dst_ref=field.at[pl.ds(target, 2)],
                send_sem=halo_send.at[turn, side],
                recv_sem=halo_recv.at[turn, side],
                device_id=(left, right)[side],
                device_id_type=MESH,
            )
            copy.start()
            copies.append(copy)
        started.extend(copies)
        return copies

    def landed(copies):
        for copy in copies:
            copy.wait_recv()

    def screened(field):
        return screen(field.reshape(CELLS, COLS), *tables).reshape(PLANES, ROWS, COLS)

    def smooth(part, planes):
        return stencil(part, planes, stiff_ref, mass_ref)

    def four(ref, at):
        return [ref[at + k] for k in range(PLANES)]

    def beside(field, added):
        planes = [field[k] for k in (0, 1, 6, 7)]
        if added is not None:
            planes = [p + outward[k] for k, p in enumerate(planes)]
        return [jnp.where(first, 0.0, p) for p in planes[0:2]] + [jnp.where(last, 0.0, p) for p in planes[2:4]]

    def fold(value):
        return value.reshape(CELLS // 8, 8, COLS)

    def dot(a, b):
        return jnp.sum(fold(a) * fold(b), axis=0)

    copies = send(guess, 0)
    for peer in lines["y"]:
        pl.semaphore_signal(entered.at[0], inc=1, device_id=peer, device_id_type=MESH)
    own = smooth(own_part, four(guess, 2))
    loads[5].wait()
    for k in range(PLANES):
        known[2 + k] = right_ref[k] - own[k]
    known[2:6] = known[2:6] - screened(guess[2:6])
    edge = send(known, 1)
    added = smooth(outward_part, four(guess, 2))
    for k in range(PLANES):
        outward[k] = -added[k]

    landed(copies)
    added = smooth(cross_part, beside(guess, None))
    for k in range(PLANES):
        residual[k] = known[2 + k] - added[k]
    own = smooth(own_part, four(residual, 0))
    for k in range(PLANES):
        partial[2 + k] = own[k]
    partial[2:6] = partial[2:6] + screened(residual[...])
    copies = send(partial, 2)
    pl.semaphore_wait(entered.at[0], len(lines["y"]))
    for peer in lines["x"]:
        pl.semaphore_signal(entered.at[1], inc=1, device_id=peer, device_id_type=MESH)

    landed(edge)
    added = smooth(cross_part, beside(known, outward))
    for k in range(PLANES):
        image[k] = partial[2 + k] + added[k]
    added = smooth(outward_part, four(residual, 0))
    for k in range(PLANES):
        outward[k] = added[k]
    own = smooth(own_part, four(image, 0))
    for k in range(PLANES):
        second[k] = own[k]
    second[...] = second[...] + screened(image[...])

    scale = jnp.max(jnp.max(jnp.abs(fold(residual[...])), axis=0), axis=0, keepdims=True)
    scale = jnp.maximum(jnp.max(scale, axis=1, keepdims=True), 1e-30)
    inverse = 1.0 / scale
    r0 = residual[...] * inverse
    w = image[...] * inverse
    u = second[...] * inverse
    groups = lane_groups()
    row = jnp.where(lax.broadcasted_iota(jnp.int32, (1, COLS), 1) >= 64, scale, 0.0)
    for group, a, b in zip(groups, (r0, r0, w), (r0, w, w)):
        row = jnp.where(group, folded(jnp.sum(dot(a, b), axis=0, keepdims=True), 8), row)
    last_moment = dot(w, u)

    added = smooth(outward_part, four(image, 0))
    for k in range(PLANES):
        weighed[k] = added[k] * inverse

    landed(copies)
    halo = beside(partial, outward)
    for k in range(PLANES):
        last_moment = last_moment + jnp.sum(
            ((halo[k] * inverse) * weighed[k]).reshape(ROWS // 8, 8, COLS), axis=0
        )
    row = jnp.where(groups[3], folded(jnp.sum(last_moment, axis=0, keepdims=True), 32), row)
    pl.semaphore_wait(entered.at[1], len(lines["x"]))

    for turn, arrived in enumerate(arrivals):
        count = len(peers[turn])
        sums[turn] = row
        arrived[count : count + 1, :] = row
        for slot, peer in enumerate(peers[turn]):
            pltpu.make_async_remote_copy(
                src_ref=sums.at[turn],
                dst_ref=arrived.at[pl.ds(slot, 1)],
                send_sem=sum_send.at[turn],
                recv_sem=sum_recv.at[turn],
                device_id=peer,
                device_id_type=MESH,
            ).start()
        if turn == len(STAGES) - 1:
            added = smooth(cross_part, beside(partial, outward))
            for k in range(PLANES):
                second[k] = second[k] + added[k]
        whole = arrived.at[pl.ds(0, count)]
        pltpu.make_async_copy(whole, whole, sum_recv.at[turn]).wait()
        row = combine(arrived[...])

    m0, m1, m2, m3 = (jnp.sum(jnp.where(group, row, 0.0), axis=1, keepdims=True) for group in groups)
    a0 = m0 / m1
    g = a0 * (m2 / m1)
    a1 = (g - 1.0) * m1 / (a0 * m3 - g * m2)
    c1 = a0 + a1 * g
    c2 = a1 * a0
    out_first[...] = jnp.broadcast_to(c1, (1, COLS))
    out_second[...] = jnp.broadcast_to(c2, (1, COLS))

    for copy in started:
        copy.wait_send()
    for turn, arrived in enumerate(arrivals):
        whole = arrived.at[pl.ds(0, len(peers[turn]))]
        pltpu.make_async_copy(whole, whole, sum_send.at[turn]).wait()


def body(right_side, initial_guess, point_cell, point_offset, point_weight, point_mask, block_count):
    slab = pltpu.VMEM((PLANES, ROWS, COLS), jnp.float32)
    vmem = pl.BlockSpec(memory_space=pltpu.VMEM)
    groups = []
    for axes in STAGES:
        size = 1
        for axis in axes:
            size *= SIZES[axis]
        groups.append(size)
    r0, w, u, c1, c2 = pl.pallas_call(
        kernel,
        out_shape=(slab, slab, slab) + (pltpu.VMEM((1, COLS), jnp.float32),) * 2,
        in_specs=[pl.BlockSpec(memory_space=pltpu.HBM)] * 6 + [vmem],
        out_specs=(vmem,) * 5,
        scratch_shapes=[
            pltpu.VMEM((PLANES, ROWS, COLS), jnp.float32),
            pltpu.VMEM((3, POINTS), jnp.int32),
            pltpu.VMEM((3, POINTS), jnp.float32),
            pltpu.VMEM((POINTS // COLS, COLS), jnp.float32),
            pltpu.VMEM((POINTS // COLS, COLS), jnp.int32),
            pltpu.VMEM((PLANES + 4, ROWS, COLS), jnp.float32),
            pltpu.VMEM((PLANES + 4, ROWS, COLS), jnp.float32),
            pltpu.VMEM((PLANES + 4, ROWS, COLS), jnp.float32),
            pltpu.VMEM((PLANES, ROWS, COLS), jnp.float32),
            pltpu.VMEM((PLANES, ROWS, COLS), jnp.float32),
            pltpu.VMEM((PLANES, ROWS + 2 * EDGE, COLS), jnp.float32),
            pltpu.VMEM((PLANES, ROWS + 2 * EDGE, COLS), jnp.float32),
            pltpu.VMEM((2 * COLS, POINTS), jnp.bfloat16),
            pltpu.VMEM((ROWS, POINTS), jnp.float32),
            pltpu.VMEM((8, POINTS), jnp.float32),
            pltpu.VMEM((8, POINTS), jnp.float32),
            pltpu.VMEM((2 * CELLS, 2 * COLS), jnp.bfloat16),
            pltpu.VMEM((2 * CELLS, POINTS), jnp.bfloat16),
            pltpu.SemaphoreType.DMA((6,)),
            pltpu.SemaphoreType.DMA((3, 2)),
            pltpu.SemaphoreType.DMA((3, 2)),
            pltpu.SemaphoreType.DMA((len(STAGES),)),
            pltpu.SemaphoreType.DMA((len(STAGES),)),
            pltpu.SemaphoreType.REGULAR((2,)),
            pltpu.VMEM((len(STAGES), 1, COLS), jnp.float32),
        ]
        + [pltpu.VMEM((size, COLS), jnp.float32) for size in groups],
        compiler_params=pltpu.CompilerParams(
            collective_id=0, has_side_effects=True, vmem_limit_bytes=56 * 1024 * 1024
        ),
        cost_estimate=pl.CostEstimate(flops=3_000_000_000, bytes_accessed=700_000, transcendentals=0),
    )(
        right_side, initial_guess, point_cell, point_offset,
        point_weight.reshape(POINTS // COLS, COLS), point_mask.reshape(POINTS // COLS, COLS), block_count.reshape(1, 1),
    )
    return initial_guess + c1 * r0 - c2 * w, r0 - c1 * w + c2 * u


def solution(mesh):
    placed = (
        P(("bricks", "pts"), None, None),
        P(("bricks", "pts"), None, None),
        P(None, ("bricks", "pts")),
        P(None, ("bricks", "pts")),
        P(("bricks", "pts")),
        P(("bricks", "pts")),
        P(("bricks", "pts")),
    )
    return jax.shard_map(
        body,
        mesh=mesh,
        in_specs=placed,
        out_specs=(P(("bricks", "pts"), None, None), P(("bricks", "pts"), None, None)),
        check_vma=False,
    )
```
